32 devices in a mesh: pipe: 4 (over x, core), dp: 4 (over z), tensor: 2 (over y).
Axes of the slice: x: 2, y: 2, z: 4, core: 2. Of those that a mesh axis runs over, the one named last changes fastest.
Arguments:
- hidden_states: bfloat16 [4, 1024, 8192], P('pipe', 'dp'), may hold values from -60 to 60
- norm_gain: bfloat16 [4, 8192], P('pipe'), may hold values from 0.5 to 2
- key_weight: bfloat16 [4, 8192, 512], P('pipe', 'dp', 'tensor'), may hold values from -0.0625 to 0.0625
- value_weight: bfloat16 [4, 8192, 512], P('pipe', 'dp', 'tensor'), may hold values from -0.0625 to 0.0625
- queries: bfloat16 [4, 1024, 4096], P('pipe', 'dp', 'tensor'), may hold values from -128 to 128
- context_cotangent: bfloat16 [4, 1024, 4096], P('pipe', 'dp', 'tensor'), may hold values from -96 to 96
- lengths: int32 [4, 4], P('pipe', 'dp'), may hold values from 64 to 256, as said below
- policy_logp: float32 [4, 4], P('pipe', 'dp'), may hold values from -90 to -30
- reference_logp: float32 [4, 4], P('pipe', 'dp'), may hold values from -90 to -30
Outputs:
- key_weight_grad: bfloat16 [4, 8192, 512], P('pipe', 'dp', 'tensor')
- value_weight_grad: bfloat16 [4, 8192, 512], P('pipe', 'dp', 'tensor')
- lower_cotangent: bfloat16 [4, 1024, 8192], P('pipe', 'dp')
The draws below stay inside these ranges and needn't reach their ends.
Inputs may be any that keep to these rules, and one draw needn't show every extreme that they name: `lengths`: each sequence's live tokens; positions at or beyond it are padding.
All inputs are finite; a program needn't handle non-finite values.
Results may differ from the reference program's by a relative error of at most 0.015.
The reference program's roundings to bfloat16 on the way count: a program that leaves them out, or rounds other values in their place, can miss the bound.
Values may be sent and summed in bfloat16 or wider, within the bound.
A program may use at most 128 MiB of HBM per device.

```python
import math
import jax
import jax.numpy as jnp
from jax import lax

D = 8192
HD = 128
HQ = 32
KVH = 4
LEN = 256
TOK_DEV = 256
SEQS = 4
TOKENS = 1024
N_PIPE = 4
N_DP = 4
N_TENSOR = 2


def draw_hidden_states(key, part):
    key_base = jax.random.fold_in(key, 11)
    key_rows = jax.random.fold_in(key, 12)
    key_cols = jax.random.fold_in(key, 13)
    shape = (N_PIPE, TOKENS, D)
    row_scale = jnp.exp(jax.random.uniform(key_rows, (N_PIPE, TOKENS, 1), jnp.float32, jnp.log(0.1), 0.0))
    col_scale = jnp.exp(jax.random.uniform(key_cols, (1, 1, D), jnp.float32, 0.0, jnp.log(10.0)))
    base = jnp.clip(jax.random.normal(key_base, shape, jnp.float32), -6.0, 6.0)
    return (base * row_scale * col_scale).astype(jnp.bfloat16)


def draw_queries(key, part):
    key_base = jax.random.fold_in(key, 21)
    shape = (N_PIPE, TOKENS, HQ * HD)
    return jnp.clip(jax.random.normal(key_base, shape, jnp.float32), -4.0, 4.0).astype(jnp.bfloat16)


def draw_lengths(key, part):
    key_vals = jax.random.fold_in(key, 31)
    key_spot = jax.random.fold_in(key, 32)
    count = N_PIPE * SEQS
    drawn = jax.random.randint(key_vals, (count,), LEN // 4, LEN + 1, jnp.int32)
    spot = jax.random.randint(key_spot, (), 0, count, jnp.int32)
    place = jnp.arange(count, dtype=jnp.int32)
    drawn = jnp.where(place == spot, LEN, drawn)
    drawn = jnp.where(place == (spot + 1) % count, LEN // 4, drawn)
    return drawn.reshape(N_PIPE, SEQS)


def shard_levels(own_key, dims, split, least, top_value):
    factor_of, own = 1.0, jax.random.fold_in(own_key, 6)
    for axis_at, parts in split:
        heights = jnp.exp(jax.random.uniform(jax.random.fold_in(own, axis_at), (parts,), jnp.float32, least / len(split), top_value / len(split)))
        factor_of = factor_of * jnp.repeat(heights, dims[axis_at] // parts).reshape([-1 if axis == axis_at else 1 for axis in range(len(dims))])
    return factor_of


def scatter_about(own_key, shape, spread, most, cuts=(), held_as=jnp.bfloat16):
    entries = spread * jax.random.normal(own_key, shape, jnp.float32)
    if cuts:
        entries = entries * shard_levels(own_key, shape, cuts, -0.22, 0.18)
    return jnp.clip(entries, -most, most).astype(held_as)


def setup_inputs(seed: int = 0) -> dict:
    key_list = jax.random.split(jax.random.key(seed), 10)
    return {
        "hidden_states": draw_hidden_states(jax.random.fold_in(key_list[9], 71), 0),
        "norm_gain": jnp.clip(jnp.exp(math.log(2.0) - 1.3862944 * jax.random.uniform(key_list[1], (N_PIPE, D), jnp.float32) ** shard_levels(key_list[1], (N_PIPE, D), ((0, 4),), -0.2, 0.2)), 0.5, 2.0).astype(jnp.bfloat16),
        "key_weight": scatter_about(key_list[2], (N_PIPE, D, KVH * HD), D ** -0.5, 0.0625, ((0, 4), (1, 4), (2, 2))),
        "value_weight": scatter_about(key_list[3], (N_PIPE, D, KVH * HD), D ** -0.5, 0.0625, ((0, 4), (1, 4), (2, 2))),
        "queries": draw_queries(jax.random.fold_in(key_list[9], 71), 0),
        "context_cotangent": scatter_about(key_list[5], (N_PIPE, TOKENS, HQ * HD), 16.0, 96.0, ((0, 4), (1, 4), (2, 2))),
        "lengths": draw_lengths(jax.random.fold_in(key_list[9], 71), 0),
        "policy_logp": jnp.clip(-90.0 + 60.0 * jax.random.uniform(key_list[7], (N_PIPE, SEQS), jnp.float32) ** shard_levels(key_list[7], (N_PIPE, SEQS), ((0, 4), (1, 4)), -0.2, 0.2), -90.0, -30.0),
        "reference_logp": jnp.clip(-90.0 + 60.0 * jax.random.uniform(key_list[8], (N_PIPE, SEQS), jnp.float32) ** shard_levels(key_list[8], (N_PIPE, SEQS), ((0, 4), (1, 4)), -0.2, 0.2), -90.0, -30.0),
    }


npo_beta = 0.1
norm_eps = 1e-05
rope_base = 500000.0

def rope_tables(length, head_dim):
    positions = jnp.arange(length).astype(jnp.float32)
    freq_index = jnp.arange(head_dim // 2).astype(jnp.float32)
    inverse = 1.0 / rope_base ** (2.0 * freq_index / head_dim)
    angles = positions[:, None] * inverse[None, :]
    cosine = jnp.concatenate([jnp.cos(angles), jnp.cos(angles)], axis=1)
    sine = jnp.concatenate([jnp.sin(angles), jnp.sin(angles)], axis=1)
    return (cosine, sine)

def rotate_half(values):
    half = values.shape[-1] // 2
    return jnp.concatenate([-values[..., half:], values[..., :half]], axis=-1)

def rotate_back(values):
    half = values.shape[-1] // 2
    return jnp.concatenate([values[..., half:], -values[..., :half]], axis=-1)

def sequence_grads(query_seq, key_seq, value_seq, cotan_seq, length_seq, cosine, sine):
    seq_len, kv_heads, head_dim = key_seq.shape
    group = query_seq.shape[1] // kv_heads
    scale = 1.0 / math.sqrt(head_dim)
    query_f = query_seq.reshape(seq_len, kv_heads, group, head_dim).astype(jnp.float32)
    cotan_f = cotan_seq.reshape(seq_len, kv_heads, group, head_dim).astype(jnp.float32)
    key_f = key_seq.astype(jnp.float32)
    value_f = value_seq.astype(jnp.float32)
    scores = jnp.einsum('ikgd,jkd->kgij', query_f, key_f) * scale
    row_pos = jnp.arange(seq_len)[:, None]
    col_pos = jnp.arange(seq_len)[None, :]
    allowed = (col_pos <= row_pos) & (col_pos < length_seq)
    scores = jnp.where(allowed, scores, -1e+30)
    highest = lax.optimization_barrier(jnp.max(scores, axis=-1, keepdims=True))
    expd = jnp.where(allowed, jnp.exp(scores - highest), 0.0)
    probs = expd / lax.optimization_barrier(jnp.sum(expd, axis=-1, keepdims=True))
    probs_low = probs.astype(jnp.bfloat16)
    value_grad = jnp.einsum('kgij,ikgd->jkd', probs_low.astype(jnp.float32), cotan_f).astype(jnp.bfloat16)
    prob_grad = jnp.einsum('ikgd,jkd->kgij', cotan_f, value_f)
    centre = lax.optimization_barrier(jnp.sum(probs * prob_grad, axis=-1, keepdims=True))
    score_grad = (probs * (prob_grad - centre) * scale).astype(jnp.bfloat16)
    rotated_grad = jnp.einsum('kgij,ikgd->jkd', score_grad.astype(jnp.float32), query_f)
    key_grad = rotated_grad * cosine[:, None, :] + rotate_back(rotated_grad * sine[:, None, :])
    return (key_grad.astype(jnp.bfloat16), value_grad)

def section_backward(hidden, gain, key_w, value_w, query_all, cotan, lens, logp, logp_ref):
    hidden_f = hidden.astype(jnp.float32)
    inv_rms = lax.rsqrt(lax.optimization_barrier(jnp.mean(hidden_f * hidden_f, axis=-1, keepdims=True)) + norm_eps)
    nhat = hidden_f * inv_rms
    gain_f = gain.astype(jnp.float32)
    normed = (nhat * gain_f).astype(jnp.bfloat16)
    key_raw = jnp.dot(normed, key_w, preferred_element_type=jnp.float32)
    values = jnp.dot(normed, value_w, preferred_element_type=jnp.float32).astype(jnp.bfloat16)
    cosine, sine = rope_tables(LEN, HD)
    key_four = key_raw.reshape(SEQS, LEN, KVH, HD)
    keys = (key_four * cosine[None, :, None, :] + rotate_half(key_four) * sine[None, :, None, :]).astype(jnp.bfloat16)
    seq_weight = 2.0 * jax.nn.sigmoid(npo_beta * (logp - logp_ref)) / SEQS
    live = jnp.arange(LEN)[None, :] < lens[:, None]
    factor = jnp.where(live, seq_weight[:, None], 0.0)
    scaled = (cotan.reshape(SEQS, LEN, HQ, HD).astype(jnp.float32) * factor[:, :, None, None]).astype(jnp.bfloat16)

    def one_sequence(items):
        return sequence_grads(items[0], items[1], items[2], items[3], items[4], cosine, sine)
    key_grad, value_grad = lax.map(one_sequence, (query_all.reshape(SEQS, LEN, HQ, HD), keys, values.reshape(SEQS, LEN, KVH, HD), scaled, lens))
    key_grad = key_grad.reshape(TOKENS, KVH * HD)
    value_grad = value_grad.reshape(TOKENS, KVH * HD)
    combined = jnp.concatenate([key_grad, value_grad], axis=1)

    def add_partial(total, pieces):
        partial_sum = lax.dot_general(pieces[0], pieces[1], (((0,), (0,)), ((), ())), preferred_element_type=jnp.float32)
        rounded = lax.optimization_barrier(partial_sum.astype(jnp.bfloat16))
        return (total + rounded.astype(jnp.float32), None)
    grad_total, unused = lax.scan(add_partial, jnp.zeros((D, 2 * KVH * HD), jnp.float32), (normed.reshape(N_DP, TOK_DEV, D), combined.reshape(N_DP, TOK_DEV, 2 * KVH * HD)))
    grad_low = grad_total.astype(jnp.bfloat16)
    width = KVH * HD // N_TENSOR
    normed_grad = jnp.zeros((TOKENS, D), jnp.float32)
    for member in range(N_TENSOR):
        lo_col = member * width
        part = lax.dot_general(key_grad[:, lo_col:lo_col + width], key_w[:, lo_col:lo_col + width], (((1,), (1,)), ((), ())), preferred_element_type=jnp.float32)
        part = part + lax.dot_general(value_grad[:, lo_col:lo_col + width], value_w[:, lo_col:lo_col + width], (((1,), (1,)), ((), ())), preferred_element_type=jnp.float32)
        normed_grad = normed_grad + lax.optimization_barrier(part.astype(jnp.bfloat16)).astype(jnp.float32)
    gain_grad_in = normed_grad * gain_f
    centre = lax.optimization_barrier(jnp.mean(gain_grad_in * nhat, axis=-1, keepdims=True))
    section_cot = ((gain_grad_in - nhat * centre) * inv_rms).astype(jnp.bfloat16)
    return (grad_low[:, :KVH * HD], grad_low[:, KVH * HD:], section_cot)

def reference(hidden_states, norm_gain, key_weight, value_weight, queries, context_cotangent, lengths, policy_logp, reference_logp):
    key_grads = []
    value_grads = []
    section_cots = []
    for section in range(N_PIPE):
        key_part, value_part, section_cot = section_backward(hidden_states[section], norm_gain[section], key_weight[section], value_weight[section], queries[section], context_cotangent[section], lengths[section], policy_logp[section], reference_logp[section])
        key_grads.append(key_part)
        value_grads.append(value_part)
        section_cots.append(section_cot)
    section_cots.append(jnp.zeros((TOKENS, D), jnp.bfloat16))
    lower = jnp.stack(section_cots[1:], axis=0)
    return (jnp.stack(key_grads, axis=0), jnp.stack(value_grads, axis=0), lower)
```

```python
import functools
import math

import jax
import jax.numpy as jnp
from jax import lax
from jax.experimental import pallas as pl
from jax.experimental.pallas import tpu as pltpu
from jax.sharding import PartitionSpec as P

HD = 128


npo_beta = 0.1
norm_eps = 1e-05
rope_base = 500000.0


def rope_tables(length, head_dim):
    positions = jnp.arange(length).astype(jnp.float32)
    freq_index = jnp.arange(head_dim // 2).astype(jnp.float32)
    inverse = 1.0 / rope_base ** (2.0 * freq_index / head_dim)
    angles = positions[:, None] * inverse[None, :]
    cosine = jnp.concatenate([jnp.cos(angles), jnp.cos(angles)], axis=1)
    sine = jnp.concatenate([jnp.sin(angles), jnp.sin(angles)], axis=1)
    return (cosine, sine)


def rotate_half(values):
    half = values.shape[-1] // 2
    return jnp.concatenate([-values[..., half:], values[..., :half]], axis=-1)


def rotate_back(values):
    half = values.shape[-1] // 2
    return jnp.concatenate([values[..., half:], -values[..., :half]], axis=-1)


def sequence_grads(query_seq, key_seq, value_seq, cotan_seq, length_seq, cosine, sine):
    seq_len, kv_heads, head_dim = key_seq.shape
    group = query_seq.shape[1] // kv_heads
    scale = 1.0 / math.sqrt(head_dim)
    query_g = query_seq.reshape(seq_len, kv_heads, group, head_dim)
    cotan_g = cotan_seq.reshape(seq_len, kv_heads, group, head_dim)
    scores = (
        jnp.einsum("ikgd,jkd->kgij", query_g, key_seq, preferred_element_type=jnp.float32) * scale
    )
    row_pos = jnp.arange(seq_len)[:, None]
    col_pos = jnp.arange(seq_len)[None, :]
    allowed = (col_pos <= row_pos) & (col_pos < length_seq)
    scores = jnp.where(allowed, scores, -1e30)
    highest = jnp.max(scores, axis=-1, keepdims=True)
    expd = jnp.where(allowed, jnp.exp(scores - highest), 0.0)
    probs = expd / jnp.sum(expd, axis=-1, keepdims=True)
    probs_low = probs.astype(jnp.bfloat16)
    value_grad = jnp.einsum(
        "kgij,ikgd->jkd", probs_low, cotan_g, preferred_element_type=jnp.float32
    ).astype(jnp.bfloat16)
    prob_grad = jnp.einsum("ikgd,jkd->kgij", cotan_g, value_seq, preferred_element_type=jnp.float32)
    centre = jnp.sum(probs * prob_grad, axis=-1, keepdims=True)
    score_grad = (probs * (prob_grad - centre) * scale).astype(jnp.bfloat16)
    rotated_grad = jnp.einsum(
        "kgij,ikgd->jkd", score_grad, query_g, preferred_element_type=jnp.float32
    )
    key_grad = rotated_grad * cosine[:, None, :] + rotate_back(rotated_grad * sine[:, None, :])
    return (key_grad.astype(jnp.bfloat16), value_grad)


MESH = pl.DeviceIdType.MESH
VMEM_BYTES = 52 * 1024 * 1024


def remote(src, dst, send_sem, recv_sem, **where):
    return pltpu.make_async_remote_copy(
        src_ref=src, dst_ref=dst, send_sem=send_sem, recv_sem=recv_sem,
        device_id=where, device_id_type=MESH,
    )


def dot_nt(left, right):
    return lax.dot_general(
        left, right, (((1,), (1,)), ((), ())), preferred_element_type=jnp.float32
    )


def dot_tn(left, right):
    return lax.dot_general(
        left, right, (((0,), (0,)), ((), ())), preferred_element_type=jnp.float32
    )


FWD_CHUNKS = 2


def project_kernel(
    count, hid, gain, kw, vw,
    cols_out, woth, inv_out, key_out, val_out,
    normed, cols, total, psend, precv,
    zs, zr, ws, wr, fs, fr, ps, pr, ls,
):
    z = lax.axis_index("dp")
    y = lax.axis_index("tensor")
    other = 1 - y
    toks, width = hid.shape
    rows = width // count
    half_rows = rows // 2
    half = toks // 2
    chunk = half // FWD_CHUNKS
    kcols = kw.shape[1]

    barrier = pltpu.get_barrier_semaphore()
    for d in range(1, count):
        pl.semaphore_signal(
            barrier, inc=1, device_id={"dp": lax.rem(z + d, count)}, device_id_type=MESH
        )
    pl.semaphore_signal(barrier, inc=1, device_id={"tensor": other}, device_id_type=MESH)
    pl.semaphore_wait(barrier, count)

    def norm_half(which):
        def step(i, carry):
            at = pl.ds(pl.multiple_of(which * half + i * 16, 16), 16)
            h = hid[at, :].astype(jnp.float32)
            inv = lax.rsqrt(jnp.mean(h * h, axis=-1, keepdims=True) + norm_eps)
            normed[at, :] = (h * inv * gain[...]).astype(jnp.bfloat16)
            inv_out[at, :] = jnp.broadcast_to(inv, (16, 128))
            return carry

        lax.fori_loop(0, half // 16, step, 0)

    def rows_of(which, c):
        return pl.ds(pl.multiple_of(which * half + c * chunk, 16), chunk)

    norm_half(y)
    sent = []
    for c in range(FWD_CHUNKS):
        for d in range(1, count):
            to = lax.rem(z + d, count)
            copy = remote(
                normed.at[rows_of(y, c), pl.ds(pl.multiple_of(to * rows, 128), rows)],
                cols.at[z, rows_of(y, c), :],
                zs.at[c, d - 1], zr.at[c, d - 1], dp=to,
            )
            copy.start()
            sent.append(copy)
    give = pl.ds(pl.multiple_of(other * half_rows, 16), half_rows)
    wcopies = [
        remote(kw.at[give, :], woth.at[0], ws.at[0], wr.at[0], tensor=other),
        remote(vw.at[give, :], woth.at[1], ws.at[1], wr.at[1], tensor=other),
    ]
    for copy in wcopies:
        copy.start()
    norm_half(other)
    own = pltpu.make_async_copy(
        normed.at[:, pl.ds(pl.multiple_of(z * rows, 128), rows)], cols.at[z], ls.at[count]
    )
    own.start()
    own.wait()

    step_k = min(rows, 512)

    def project(src, c):
        def step(k, acc):
            at = pl.ds(pl.multiple_of(k * step_k, 128), step_k)
            a = jnp.concatenate(
                [cols[src, pl.ds(c * chunk, chunk), at], cols[src, pl.ds(half + c * chunk, chunk), at]],
                axis=0,
            )
            return (
                acc[0] + jnp.dot(a, kw[at, :], preferred_element_type=jnp.float32),
                acc[1] + jnp.dot(a, vw[at, :], preferred_element_type=jnp.float32),
            )

        zero = jnp.zeros((2 * chunk, kcols), jnp.float32)
        return lax.fori_loop(0, rows // step_k, step, (zero, zero))

    for c in range(FWD_CHUNKS):
        ka, va = project(z, c)
        total[c, :, :kcols] = ka
        total[c, :, kcols:] = va
    outs = []
    copy = pltpu.make_async_copy(cols.at[z], cols_out.at[z], ls.at[0])
    copy.start()
    outs.append(copy)

    for c in range(FWD_CHUNKS):
        for d in range(1, count):
            src = lax.rem(z - d + count, count)
            place = cols.at[src, rows_of(y, c), :]
            remote(place, place, zs.at[c, d - 1], zr.at[c, d - 1], dp=src).wait_recv()
            copy = remote(place, place, fs.at[c, d - 1], fr.at[c, d - 1], tensor=other)
            copy.start()
            sent.append(copy)
        for d in range(1, count):
            src = lax.rem(z - d + count, count)
            place = cols.at[src, rows_of(other, c), :]
            remote(place, place, fs.at[c, d - 1], fr.at[c, d - 1], tensor=other).wait_recv()
            ka, va = project(src, c)
            psend[d - 1, c, :, :kcols] = ka.astype(jnp.bfloat16)
            psend[d - 1, c, :, kcols:] = va.astype(jnp.bfloat16)
            copy = remote(
                psend.at[d - 1, c], precv.at[d - 1, c], ps.at[c, d - 1], pr.at[c, d - 1], dp=src
            )
            copy.start()
            sent.append(copy)
            if c == FWD_CHUNKS - 1:
                copy = pltpu.make_async_copy(cols.at[src], cols_out.at[src], ls.at[d])
                copy.start()
                outs.append(copy)
    for c in range(FWD_CHUNKS):
        acc = total[c]
        for d in range(1, count):
            remote(
                psend.at[d - 1, c], precv.at[d - 1, c], ps.at[c, d - 1], pr.at[c, d - 1],
                dp=lax.rem(z + d, count),
            ).wait_recv()
            acc = acc + precv[d - 1, c].astype(jnp.float32)
        for which in range(2):
            at = pl.ds(which * half + c * chunk, chunk)
            part = acc[which * chunk : (which + 1) * chunk]
            key_out[at, :] = part[:, :kcols]
            val_out[at, :] = part[:, kcols:]
    for copy in sent:
        copy.wait_send()
    for copy in wcopies:
        copy.wait()
    for copy in outs:
        copy.wait()


def project_call(hidden, gain_f, kw, vw, count):
    toks, width = hidden.shape
    rows = width // count
    kcols = kw.shape[1]
    vmem = pl.BlockSpec(memory_space=pltpu.VMEM)
    hbm = pl.BlockSpec(memory_space=pl.ANY)
    dma = pltpu.SemaphoreType.DMA
    m = 2 * (toks // 2 // FWD_CHUNKS)
    pair = (FWD_CHUNKS, count - 1)
    return pl.pallas_call(
        functools.partial(project_kernel, count),
        out_shape=(
            jax.ShapeDtypeStruct((count, toks, rows), jnp.bfloat16),
            jax.ShapeDtypeStruct((2, rows // 2, kcols), jnp.bfloat16),
            jax.ShapeDtypeStruct((toks, 128), jnp.float32),
            jax.ShapeDtypeStruct((toks, kcols), jnp.float32),
            jax.ShapeDtypeStruct((toks, kcols), jnp.float32),
        ),
        in_specs=[vmem] * 4,
        out_specs=(hbm, hbm, vmem, vmem, vmem),
        scratch_shapes=[
            pltpu.VMEM((toks, width), jnp.bfloat16),
            pltpu.VMEM((count, toks, rows), jnp.bfloat16),
            pltpu.VMEM((FWD_CHUNKS, m, 2 * kcols), jnp.float32),
            pltpu.VMEM((count - 1, FWD_CHUNKS, m, 2 * kcols), jnp.bfloat16),
            pltpu.VMEM((count - 1, FWD_CHUNKS, m, 2 * kcols), jnp.bfloat16),
            dma(pair), dma(pair), dma((2,)), dma((2,)), dma(pair), dma(pair), dma(pair), dma(pair),
            dma((count + 1,)),
        ],
        compiler_params=pltpu.CompilerParams(
            collective_id=0, has_side_effects=True, vmem_limit_bytes=VMEM_BYTES
        ),
        name="project",
    )(hidden, gain_f, kw, vw)


BWD_CHUNKS = 4


def backward_kernel(
    count, stages, comb, cpart, inv, hid, gain, kw, vw, woth, cols,
    low, kg_out, vg_out,
    pown, poth, ngs, ngr, cot, cother,
    sa, ra, sb, rb, sc, rc, sn, rn, so, ro,
):
    p = lax.axis_index("pipe")
    z = lax.axis_index("dp")
    y = lax.axis_index("tensor")
    other = 1 - y
    toks, width = hid.shape
    rows = width // count
    half_rows = rows // 2
    kcols = kw.shape[1]
    chunk = toks // BWD_CHUNKS
    has_lower = p > 0
    has_upper = p < stages - 1

    barrier = pltpu.get_barrier_semaphore()
    for d in range(1, count):
        pl.semaphore_signal(
            barrier, inc=1, device_id={"dp": lax.rem(z + d, count)}, device_id_type=MESH
        )
    pl.semaphore_signal(barrier, inc=1, device_id={"tensor": other}, device_id_type=MESH)
    for t in range(2):

        @pl.when(has_lower)
        def _():
            pl.semaphore_signal(
                barrier, inc=1, device_id={"pipe": p - 1, "tensor": t}, device_id_type=MESH
            )

        @pl.when(has_upper)
        def _():
            pl.semaphore_signal(
                barrier, inc=1, device_id={"pipe": p + 1, "tensor": t}, device_id_type=MESH
            )

    peers = count + 2 * has_lower.astype(jnp.int32) + 2 * has_upper.astype(jnp.int32)
    pl.semaphore_wait(barrier, peers)

    sent = []
    for d in range(1, count):
        copy = remote(comb, pown.at[z], sa.at[d - 1], ra.at[d - 1], dp=lax.rem(z + d, count))
        copy.start()
        sent.append(copy)
    copy = remote(comb, poth.at[z], sb.at[0], rb.at[0], tensor=other)
    copy.start()
    sent.append(copy)
    ccopy = remote(cpart, cother, sc.at[0], rc.at[0], tensor=other)
    ccopy.start()
    pown[z] = comb[...]
    for d in range(1, count):
        src = lax.rem(z - d + count, count)
        remote(comb, pown.at[src], sa.at[d - 1], ra.at[d - 1], dp=src).wait_recv()
        copy = remote(pown.at[src], poth.at[src], sb.at[d], rb.at[d], tensor=other)
        copy.start()
        sent.append(copy)

    tile = min(half_rows, 256)

    def normed_grad(src, out, slot):
        def step(n, carry):
            mine = pl.ds(pl.multiple_of(y * half_rows + n * tile, 16), tile)
            at = pl.ds(pl.multiple_of(n * tile, 128), tile)
            a = dot_nt(pown[src, :, :kcols], kw[mine, :]) + dot_nt(pown[src, :, kcols:], vw[mine, :])
            b = dot_nt(poth[src, :, :kcols], woth[0, at, :]) + dot_nt(poth[src, :, kcols:], woth[1, at, :])
            both = a.astype(jnp.bfloat16).astype(jnp.float32) + b.astype(jnp.bfloat16).astype(jnp.float32)
            out[slot, :, at] = both.astype(jnp.bfloat16)
            return carry

        lax.fori_loop(0, half_rows // tile, step, 0)

    def wait_other(d):
        src = lax.rem(z - d + count, count)
        remote(pown.at[src], poth.at[src], sb.at[d], rb.at[d], tensor=other).wait_recv()

    wait_other(0)
    normed_grad(z, ngr, z)
    for d in range(1, count):
        wait_other(d)
        normed_grad(lax.rem(z - d + count, count), ngs, d - 1)
    for c in range(BWD_CHUNKS):
        at = pl.ds(c * chunk, chunk)
        for d in range(1, count):
            copy = remote(
                ngs.at[d - 1, at, :], ngr.at[z, at, :], sn.at[c, d - 1], rn.at[c, d - 1],
                dp=lax.rem(z - d + count, count),
            )
            copy.start()
            sent.append(copy)
    ccopy.wait()

    wtile = min(rows, 256)
    wsteps = rows // wtile

    def weight_grad(n, carry):
        at = pl.ds(pl.multiple_of(n * wtile, 128), wtile)
        acc = jnp.zeros((wtile, 2 * kcols), jnp.float32)
        for r in range(count):
            term = dot_tn(cols[r, :, at], pown[r])
            acc = acc + term.astype(jnp.bfloat16).astype(jnp.float32)
        low_acc = acc.astype(jnp.bfloat16)
        kg_out[at, :] = low_acc[:, :kcols]
        vg_out[at, :] = low_acc[:, kcols:]
        return carry

    def out_copy(c, w, k, up):
        at = pl.ds(c * chunk, chunk)
        half_at = y if (not up or k == 0) else other
        feat = pl.ds(pl.multiple_of(w * rows + half_at * half_rows, 128), half_rows)
        return remote(
            cot.at[w, at, :], low.at[at, feat], so.at[c, w, k], ro.at[c, w, k],
            pipe=p + 1 if up else p - 1, tensor=y if k == 0 else other,
        )

    for c in range(BWD_CHUNKS):
        lax.fori_loop(wsteps * c // BWD_CHUNKS, wsteps * (c + 1) // BWD_CHUNKS, weight_grad, 0)
        for d in range(1, count):
            to = lax.rem(z + d, count)
            remote(
                ngs.at[d - 1, pl.ds(c * chunk, chunk), :], ngr.at[to, pl.ds(c * chunk, chunk), :],
                sn.at[c, d - 1], rn.at[c, d - 1], dp=to,
            ).wait_recv()

        def tail(i, carry):
            at = pl.ds(pl.multiple_of(c * chunk + i * 16, 16), 16)
            inv_rms = inv[at, :][:, :1]
            centre = (cpart[at, :] + cother[at, :])[:, :1] * (1.0 / width)
            for w in range(count):
                feat = pl.ds(pl.multiple_of(w * rows + y * half_rows, 128), half_rows)
                nhat = hid[at, feat].astype(jnp.float32) * inv_rms
                grad_in = ngr[w, at, :].astype(jnp.float32) * gain[:, feat]
                cot[w, at, :] = ((grad_in - nhat * centre) * inv_rms).astype(jnp.bfloat16)
            return carry

        lax.fori_loop(0, chunk // 16, tail, 0)

        @pl.when(has_lower)
        def _():
            for w in range(count):
                for k in range(2):
                    out_copy(c, w, k, False).start()

    for copy in sent:
        copy.wait_send()

    @pl.when(has_lower)
    def _():
        for c in range(BWD_CHUNKS):
            for w in range(count):
                for k in range(2):
                    out_copy(c, w, k, False).wait_send()

    @pl.when(has_upper)
    def _():
        for c in range(BWD_CHUNKS):
            for w in range(count):
                for k in range(2):
                    out_copy(c, w, k, True).wait_recv()


def backward_call(comb, cpart, inv, hidden, gain_f, kw, vw, woth, cols, count, stages):
    toks, width = hidden.shape
    rows = width // count
    kcols = kw.shape[1]
    vmem = pl.BlockSpec(memory_space=pltpu.VMEM)
    hbm = pl.BlockSpec(memory_space=pl.ANY)
    dma = pltpu.SemaphoreType.DMA
    pair = (BWD_CHUNKS, count - 1)
    trio = (BWD_CHUNKS, count, 2)
    return pl.pallas_call(
        functools.partial(backward_kernel, count, stages),
        out_shape=(
            jax.ShapeDtypeStruct((toks, width), jnp.bfloat16),
            jax.ShapeDtypeStruct((rows, kcols), jnp.bfloat16),
            jax.ShapeDtypeStruct((rows, kcols), jnp.bfloat16),
        ),
        in_specs=[vmem] * 9,
        out_specs=(hbm, vmem, vmem),
        scratch_shapes=[
            pltpu.VMEM((count, toks, 2 * kcols), jnp.bfloat16),
            pltpu.VMEM((count, toks, 2 * kcols), jnp.bfloat16),
            pltpu.VMEM((count - 1, toks, rows // 2), jnp.bfloat16),
            pltpu.VMEM((count, toks, rows // 2), jnp.bfloat16),
            pltpu.VMEM((count, toks, rows // 2), jnp.bfloat16),
            pltpu.VMEM((toks, 128), jnp.float32),
            dma((count - 1,)), dma((count - 1,)), dma((count,)), dma((count,)), dma((1,)), dma((1,)),
            dma(pair), dma(pair), dma(trio), dma(trio),
        ],
        compiler_params=pltpu.CompilerParams(
            collective_id=1, has_side_effects=True, vmem_limit_bytes=VMEM_BYTES
        ),
        name="backward",
    )(comb, cpart, inv, hidden, gain_f, kw, vw, woth, cols)


def on_device(
    hidden_states,
    norm_gain,
    key_weight,
    value_weight,
    queries,
    context_cotangent,
    lengths,
    policy_logp,
    reference_logp,
):
    count = lax.axis_size("dp")
    stages = lax.axis_size("pipe")
    hidden = hidden_states[0]
    gain_f = norm_gain.astype(jnp.float32)
    kw, vw = key_weight[0], value_weight[0]
    tok_rows = hidden.shape[0]
    seq_count = lengths.shape[1]
    seq_len = tok_rows // seq_count
    kv_cols = kw.shape[1]
    kv_local = kv_cols // HD
    q_local = queries.shape[2] // HD
    cols, woth, inv, key_raw, val_raw = project_call(hidden, gain_f, kw, vw, count)
    values = val_raw.astype(jnp.bfloat16)
    cosine, sine = rope_tables(seq_len, HD)
    key_four = key_raw.reshape(seq_count, seq_len, kv_local, HD)
    keys = (
        key_four * cosine[None, :, None, :] + rotate_half(key_four) * sine[None, :, None, :]
    ).astype(jnp.bfloat16)
    total_seqs = seq_count * count
    seq_weight = 2.0 * jax.nn.sigmoid(npo_beta * (policy_logp[0] - reference_logp[0])) / total_seqs
    live = jnp.arange(seq_len)[None, :] < lengths[0][:, None]
    factor = jnp.where(live, seq_weight[:, None], 0.0)
    scaled = (
        context_cotangent[0].reshape(seq_count, seq_len, q_local, HD).astype(jnp.float32)
        * factor[:, :, None, None]
    ).astype(jnp.bfloat16)

    def one_sequence(items):
        return sequence_grads(items[0], items[1], items[2], items[3], items[4], cosine, sine)

    key_grad, value_grad = lax.map(
        one_sequence,
        (
            queries[0].reshape(seq_count, seq_len, q_local, HD),
            keys,
            values.reshape(seq_count, seq_len, kv_local, HD),
            scaled,
            lengths[0],
        ),
    )
    key_grad = key_grad.reshape(tok_rows, kv_cols)
    value_grad = value_grad.reshape(tok_rows, kv_cols)
    combined = jnp.concatenate([key_grad, value_grad], axis=1)
    cpart = jnp.sum(
        key_grad.astype(jnp.float32) * key_raw + value_grad.astype(jnp.float32) * val_raw,
        axis=-1, keepdims=True,
    )
    cpart = jnp.broadcast_to(cpart, (tok_rows, 128))
    low, kg, vg = backward_call(
        combined, cpart, inv, hidden, gain_f, kw, vw, woth, cols, count, stages
    )
    low = jnp.where(lax.axis_index("pipe") < stages - 1, low, jnp.zeros_like(low))
    return (kg[None], vg[None], low[None])


def solution(mesh):
    in_specs = (
        P("pipe", "dp", None),
        P("pipe", None),
        P("pipe", "dp", "tensor"),
        P("pipe", "dp", "tensor"),
        P("pipe", "dp", "tensor"),
        P("pipe", "dp", "tensor"),
        P("pipe", "dp"),
        P("pipe", "dp"),
        P("pipe", "dp"),
    )
    out_specs = (P("pipe", "dp", "tensor"), P("pipe", "dp", "tensor"), P("pipe", "dp", None))
    return jax.shard_map(
        on_device, mesh=mesh, in_specs=in_specs, out_specs=out_specs, check_vma=False
    )
```

```python
import functools
import math

import jax
import jax.numpy as jnp
from jax import lax
from jax.experimental import pallas as pl
from jax.experimental.pallas import tpu as pltpu
from jax.sharding import PartitionSpec as P

HD = 128


npo_beta = 0.1
norm_eps = 1e-05
rope_base = 500000.0


def rope_tables(length, head_dim):
    positions = jnp.arange(length).astype(jnp.float32)
    freq_index = jnp.arange(head_dim // 2).astype(jnp.float32)
    inverse = 1.0 / rope_base ** (2.0 * freq_index / head_dim)
    angles = positions[:, None] * inverse[None, :]
    cosine = jnp.concatenate([jnp.cos(angles), jnp.cos(angles)], axis=1)
    sine = jnp.concatenate([jnp.sin(angles), jnp.sin(angles)], axis=1)
    return (cosine, sine)


MESH = pl.DeviceIdType.MESH
VMEM_BYTES = 52 * 1024 * 1024


def remote(src, dst, send_sem, recv_sem, **where):
    return pltpu.make_async_remote_copy(
        src_ref=src, dst_ref=dst, send_sem=send_sem, recv_sem=recv_sem,
        device_id=where, device_id_type=MESH,
    )


def dot_nt(left, right):
    return lax.dot_general(
        left, right, (((1,), (1,)), ((), ())), preferred_element_type=jnp.float32
    )


def dot_tn(left, right):
    return lax.dot_general(
        left, right, (((0,), (0,)), ((), ())), preferred_element_type=jnp.float32
    )


FWD_CHUNKS = 2
BWD_CHUNKS = 4


def section_kernel(
    count, stages,
    hid, gain, kw, vw, query, cotan, factor, live, cosine, sine,
    low, kg_out, vg_out,
    normed, cols, total, psend, precv, woth, inv, key_raw, val_raw,
    comb, cpart, pown, poth, ngs, ngr, cot, cother,
    zs, zr, ws, wr, fs, fr, ps, pr, ls,
    sa, ra, sb, rb, sc, rc, sn, rn, so, ro,
):
    p = lax.axis_index("pipe")
    z = lax.axis_index("dp")
    y = lax.axis_index("tensor")
    other = 1 - y
    toks, width = hid.shape
    rows = width // count
    half_rows = rows // 2
    kcols = kw.shape[1]
    chunk = toks // BWD_CHUNKS
    half = toks // 2
    fchunk = half // FWD_CHUNKS
    has_lower = p > 0
    has_upper = p < stages - 1

    barrier = pltpu.get_barrier_semaphore()
    for d in range(1, count):
        pl.semaphore_signal(
            barrier, inc=1, device_id={"dp": lax.rem(z + d, count)}, device_id_type=MESH
        )
    pl.semaphore_signal(barrier, inc=1, device_id={"tensor": other}, device_id_type=MESH)

    @pl.when(has_lower)
    def _():
        pl.semaphore_signal(barrier, inc=1, device_id={"pipe": p - 1}, device_id_type=MESH)

    @pl.when(has_upper)
    def _():
        pl.semaphore_signal(barrier, inc=1, device_id={"pipe": p + 1}, device_id_type=MESH)

    peers = count + has_lower.astype(jnp.int32) + has_upper.astype(jnp.int32)
    pl.semaphore_wait(barrier, peers)

    def norm_half(which):
        def step(i, carry):
            at = pl.ds(pl.multiple_of(which * half + i * 16, 16), 16)
            h = hid[at, :].astype(jnp.float32)
            scale_row = lax.rsqrt(jnp.mean(h * h, axis=-1, keepdims=True) + norm_eps)
            normed[at, :] = (h * scale_row * gain[...]).astype(jnp.bfloat16)
            inv[at, :] = jnp.broadcast_to(scale_row, (16, 128))
            return carry

        lax.fori_loop(0, half // 16, step, 0)

    def rows_of(which, c):
        return pl.ds(pl.multiple_of(which * half + c * fchunk, 16), fchunk)

    norm_half(y)
    sent = []
    for c in range(FWD_CHUNKS):
        for d in range(1, count):
            to = lax.rem(z + d, count)
            copy = remote(
                normed.at[rows_of(y, c), pl.ds(pl.multiple_of(to * rows, 128), rows)],
                cols.at[z, rows_of(y, c), :],
                zs.at[c, d - 1], zr.at[c, d - 1], dp=to,
            )
            copy.start()
            sent.append(copy)
    give = pl.ds(pl.multiple_of(other * half_rows, 16), half_rows)
    wcopies = [
        remote(kw.at[give, :], woth.at[0], ws.at[0], wr.at[0], tensor=other),
        remote(vw.at[give, :], woth.at[1], ws.at[1], wr.at[1], tensor=other),
    ]
    for copy in wcopies:
        copy.start()
    norm_half(other)
    own = pltpu.make_async_copy(
        normed.at[:, pl.ds(pl.multiple_of(z * rows, 128), rows)], cols.at[z], ls.at[0]
    )
    own.start()
    own.wait()

    step_k = min(rows, 512)

    def project(src, c):
        def step(k, acc):
            at = pl.ds(pl.multiple_of(k * step_k, 128), step_k)
            a = jnp.concatenate(
                [cols[src, pl.ds(c * fchunk, fchunk), at], cols[src, pl.ds(half + c * fchunk, fchunk), at]],
                axis=0,
            )
            return (
                acc[0] + jnp.dot(a, kw[at, :], preferred_element_type=jnp.float32),
                acc[1] + jnp.dot(a, vw[at, :], preferred_element_type=jnp.float32),
            )

        zero = jnp.zeros((2 * fchunk, kcols), jnp.float32)
        return lax.fori_loop(0, rows // step_k, step, (zero, zero))

    for c in range(FWD_CHUNKS):
        ka, va = project(z, c)
        total[c, :, :kcols] = ka
        total[c, :, kcols:] = va

    for c in range(FWD_CHUNKS):
        for d in range(1, count):
            src = lax.rem(z - d + count, count)
            place = cols.at[src, rows_of(y, c), :]
            remote(place, place, zs.at[c, d - 1], zr.at[c, d - 1], dp=src).wait_recv()
            copy = remote(place, place, fs.at[c, d - 1], fr.at[c, d - 1], tensor=other)
            copy.start()
            sent.append(copy)
        for d in range(1, count):
            src = lax.rem(z - d + count, count)
            place = cols.at[src, rows_of(other, c), :]
            remote(place, place, fs.at[c, d - 1], fr.at[c, d - 1], tensor=other).wait_recv()
            ka, va = project(src, c)
            psend[d - 1, c, :, :kcols] = ka.astype(jnp.bfloat16)
            psend[d - 1, c, :, kcols:] = va.astype(jnp.bfloat16)
            copy = remote(
                psend.at[d - 1, c], precv.at[d - 1, c], ps.at[c, d - 1], pr.at[c, d - 1], dp=src
            )
            copy.start()
            sent.append(copy)
    for c in range(FWD_CHUNKS):
        acc = total[c]
        for d in range(1, count):
            remote(
                psend.at[d - 1, c], precv.at[d - 1, c], ps.at[c, d - 1], pr.at[c, d - 1],
                dp=lax.rem(z + d, count),
            ).wait_recv()
            acc = acc + precv[d - 1, c].astype(jnp.float32)
        for which in range(2):
            at = pl.ds(which * half + c * fchunk, fchunk)
            part = acc[which * fchunk : (which + 1) * fchunk]
            key_raw[at, :] = part[:, :kcols]
            val_raw[at, :] = part[:, kcols:]

    lane = lax.broadcasted_iota(jnp.int32, (toks, HD), 1)
    sign = jnp.where(lane < HD // 2, -1.0, 1.0)
    key_pos = lax.broadcasted_iota(jnp.int32, (toks, toks), 0)
    query_pos = lax.broadcasted_iota(jnp.int32, (toks, toks), 1)
    allowed = (key_pos <= query_pos) & (live[...][:, :1] > 0.0)
    bias = jnp.where(allowed, 0.0, -1e30)
    scale = 1.0 / math.sqrt(HD)
    group = query.shape[1] // kcols
    weigh = factor[...][:, :1]
    cen = jnp.zeros((toks, 1), jnp.float32)
    for k in range(kcols // HD):
        head = pl.ds(k * HD, HD)
        raw = key_raw[:, head]
        key = (raw * cosine[...] + pltpu.roll(raw, HD // 2, 1) * sign * sine[...]).astype(jnp.bfloat16)
        value = val_raw[:, head].astype(jnp.bfloat16)
        vgrad = jnp.zeros((toks, HD), jnp.float32)
        rgrad = jnp.zeros((toks, HD), jnp.float32)
        for g in range(group):
            at = pl.ds((k * group + g) * HD, HD)
            q = query[:, at]
            co = (cotan[:, at].astype(jnp.float32) * weigh).astype(jnp.bfloat16)
            scores = dot_nt(key, q) * scale + bias
            expd = jnp.exp(scores - jnp.max(scores, axis=0, keepdims=True))
            probs = expd * (1.0 / jnp.sum(expd, axis=0, keepdims=True))
            pgrad = dot_nt(value, co)
            centre = jnp.sum(probs * pgrad, axis=0, keepdims=True)
            sgrad = (probs * (pgrad - centre) * scale).astype(jnp.bfloat16)
            vgrad = vgrad + jnp.dot(probs.astype(jnp.bfloat16), co, preferred_element_type=jnp.float32)
            rgrad = rgrad + jnp.dot(sgrad, q, preferred_element_type=jnp.float32)
        kgrad = rgrad * cosine[...] - pltpu.roll(rgrad * sine[...], HD // 2, 1) * sign
        klow, vlow = kgrad.astype(jnp.bfloat16), vgrad.astype(jnp.bfloat16)
        comb[:, head] = klow
        comb[:, pl.ds(kcols + k * HD, HD)] = vlow
        cen = cen + jnp.sum(
            klow.astype(jnp.float32) * raw + vlow.astype(jnp.float32) * val_raw[:, head],
            axis=1, keepdims=True,
        )
    cpart[...] = jnp.broadcast_to(cen, (toks, 128))

    for d in range(1, count):
        copy = remote(comb, pown.at[z], sa.at[d - 1], ra.at[d - 1], dp=lax.rem(z + d, count))
        copy.start()
        sent.append(copy)
    copy = remote(comb, poth.at[z], sb.at[0], rb.at[0], tensor=other)
    copy.start()
    sent.append(copy)
    ccopy = remote(cpart, cother, sc.at[0], rc.at[0], tensor=other)
    ccopy.start()
    pown[z] = comb[...]
    for d in range(1, count):
        src = lax.rem(z - d + count, count)
        remote(comb, pown.at[src], sa.at[d - 1], ra.at[d - 1], dp=src).wait_recv()
        copy = remote(pown.at[src], poth.at[src], sb.at[d], rb.at[d], tensor=other)
        copy.start()
        sent.append(copy)

    tile = min(half_rows, 256)

    def normed_grad(src, out, slot):
        def step(n, carry):
            mine = pl.ds(pl.multiple_of(y * half_rows + n * tile, 16), tile)
            at = pl.ds(pl.multiple_of(n * tile, 128), tile)
            a = dot_nt(pown[src, :, :kcols], kw[mine, :]) + dot_nt(pown[src, :, kcols:], vw[mine, :])
            b = dot_nt(poth[src, :, :kcols], woth[0, at, :]) + dot_nt(poth[src, :, kcols:], woth[1, at, :])
            both = a.astype(jnp.bfloat16).astype(jnp.float32) + b.astype(jnp.bfloat16).astype(jnp.float32)
            out[slot, :, at] = both.astype(jnp.bfloat16)
            return carry

        lax.fori_loop(0, half_rows // tile, step, 0)

    def wait_other(d):
        src = lax.rem(z - d + count, count)
        remote(pown.at[src], poth.at[src], sb.at[d], rb.at[d], tensor=other).wait_recv()

    for copy in wcopies:
        copy.wait()
    wait_other(0)
    normed_grad(z, ngr, z)
    for d in range(1, count):
        wait_other(d)
        normed_grad(lax.rem(z - d + count, count), ngs, d - 1)
    for c in range(BWD_CHUNKS):
        at = pl.ds(c * chunk, chunk)
        for d in range(1, count):
            copy = remote(
                ngs.at[d - 1, at, :], ngr.at[z, at, :], sn.at[c, d - 1], rn.at[c, d - 1],
                dp=lax.rem(z - d + count, count),
            )
            copy.start()
            sent.append(copy)
    ccopy.wait()

    wtile = min(rows, 256)
    wsteps = rows // wtile

    def weight_grad(n, carry):
        at = pl.ds(pl.multiple_of(n * wtile, 128), wtile)
        acc = jnp.zeros((wtile, 2 * kcols), jnp.float32)
        for r in range(count):
            term = dot_tn(cols[r, :, at], pown[r])
            acc = acc + term.astype(jnp.bfloat16).astype(jnp.float32)
        low_acc = acc.astype(jnp.bfloat16)
        kg_out[at, :] = low_acc[:, :kcols]
        vg_out[at, :] = low_acc[:, kcols:]
        return carry

    def out_place(c, w, which):
        feat = pl.ds(pl.multiple_of(w * rows + which * half_rows, 128), half_rows)
        return low.at[pl.ds(c * chunk, chunk), feat]

    def out_copy(c, w, to):
        src = cot.at[w, pl.ds(c * chunk, chunk), :]
        return remote(src, out_place(c, w, y), so.at[c, w, 0], ro.at[c, w, 0], pipe=to)

    def cross_copy(c, w, which):
        place = out_place(c, w, which)
        return remote(place, place, so.at[c, w, 1], ro.at[c, w, 1], tensor=other)

    def pass_on(c):
        @pl.when(has_upper)
        def _():
            for w in range(count):
                out_copy(c, w, p + 1).wait_recv()
                cross_copy(c, w, y).start()

    for c in range(BWD_CHUNKS):
        lax.fori_loop(wsteps * c // BWD_CHUNKS, wsteps * (c + 1) // BWD_CHUNKS, weight_grad, 0)
        for d in range(1, count):
            to = lax.rem(z + d, count)
            remote(
                ngs.at[d - 1, pl.ds(c * chunk, chunk), :], ngr.at[to, pl.ds(c * chunk, chunk), :],
                sn.at[c, d - 1], rn.at[c, d - 1], dp=to,
            ).wait_recv()

        def tail(i, carry):
            at = pl.ds(pl.multiple_of(c * chunk + i * 16, 16), 16)
            inv_rms = inv[at, :][:, :1]
            centre = (cpart[at, :] + cother[at, :])[:, :1] * (1.0 / width)
            for w in range(count):
                feat = pl.ds(pl.multiple_of(w * rows + y * half_rows, 128), half_rows)
                nhat = hid[at, feat].astype(jnp.float32) * inv_rms
                grad_in = ngr[w, at, :].astype(jnp.float32) * gain[:, feat]
                cot[w, at, :] = ((grad_in - nhat * centre) * inv_rms).astype(jnp.bfloat16)
            return carry

        lax.fori_loop(0, chunk // 16, tail, 0)

        @pl.when(has_lower)
        def _():
            for w in range(count):
                out_copy(c, w, p - 1).start()

        if c > 0:
            pass_on(c - 1)

    pass_on(BWD_CHUNKS - 1)

    for copy in sent:
        copy.wait_send()

    @pl.when(has_lower)
    def _():
        for c in range(BWD_CHUNKS):
            for w in range(count):
                out_copy(c, w, p - 1).wait_send()

    @pl.when(has_upper)
    def _():
        for c in range(BWD_CHUNKS):
            for w in range(count):
                cross_copy(c, w, y).wait_send()
                cross_copy(c, w, other).wait_recv()


def section_call(arrays, count, stages):
    hidden, _, kw = arrays[:3]
    toks, width = hidden.shape
    rows = width // count
    kcols = kw.shape[1]
    low, wide = jnp.bfloat16, jnp.float32
    vmem = pl.BlockSpec(memory_space=pltpu.VMEM)
    hbm = pl.BlockSpec(memory_space=pl.ANY)
    dma = pltpu.SemaphoreType.DMA
    m = toks // FWD_CHUNKS
    fpair = (FWD_CHUNKS, count - 1)
    bpair = (BWD_CHUNKS, count - 1)
    trio = (BWD_CHUNKS, count, 2)
    others = count - 1
    return pl.pallas_call(
        functools.partial(section_kernel, count, stages),
        out_shape=(
            jax.ShapeDtypeStruct((toks, width), low),
            jax.ShapeDtypeStruct((rows, kcols), low),
            jax.ShapeDtypeStruct((rows, kcols), low),
        ),
        in_specs=[vmem] * 10,
        out_specs=(hbm, vmem, vmem),
        scratch_shapes=[
            pltpu.VMEM((toks, width), low),
            pltpu.VMEM((count, toks, rows), low),
            pltpu.VMEM((FWD_CHUNKS, m, 2 * kcols), wide),
            pltpu.VMEM((others, FWD_CHUNKS, m, 2 * kcols), low),
            pltpu.VMEM((others, FWD_CHUNKS, m, 2 * kcols), low),
            pltpu.VMEM((2, rows // 2, kcols), low),
            pltpu.VMEM((toks, 128), wide),
            pltpu.VMEM((toks, kcols), wide),
            pltpu.VMEM((toks, kcols), wide),
            pltpu.VMEM((toks, 2 * kcols), low),
            pltpu.VMEM((toks, 128), wide),
            pltpu.VMEM((count, toks, 2 * kcols), low),
            pltpu.VMEM((count, toks, 2 * kcols), low),
            pltpu.VMEM((others, toks, rows // 2), low),
            pltpu.VMEM((count, toks, rows // 2), low),
            pltpu.VMEM((count, toks, rows // 2), low),
            pltpu.VMEM((toks, 128), wide),
            dma(fpair), dma(fpair), dma((2,)), dma((2,)), dma(fpair), dma(fpair), dma(fpair), dma(fpair),
            dma((1,)),
            dma((others,)), dma((others,)), dma((count,)), dma((count,)), dma((1,)), dma((1,)),
            dma(bpair), dma(bpair), dma(trio), dma(trio),
        ],
        compiler_params=pltpu.CompilerParams(
            collective_id=0, has_side_effects=True, vmem_limit_bytes=VMEM_BYTES
        ),
        name="section",
    )(*arrays)


def on_device(
    hidden_states,
    norm_gain,
    key_weight,
    value_weight,
    queries,
    context_cotangent,
    lengths,
    policy_logp,
    reference_logp,
):
    count = lax.axis_size("dp")
    stages = lax.axis_size("pipe")
    hidden = hidden_states[0]
    toks = hidden.shape[0]
    assert lengths.shape[1] == 1 and lax.axis_size("tensor") == 2
    cosine, sine = rope_tables(toks, HD)
    seq_weight = 2.0 * jax.nn.sigmoid(npo_beta * (policy_logp[0] - reference_logp[0])) / count
    live = jnp.arange(toks)[:, None] < lengths[0][None, :]
    factor = jnp.where(live, seq_weight[None, :], 0.0)
    low, kg, vg = section_call(
        (
            hidden,
            norm_gain.astype(jnp.float32),
            key_weight[0],
            value_weight[0],
            queries[0],
            context_cotangent[0],
            jnp.broadcast_to(factor, (toks, 128)),
            jnp.broadcast_to(live.astype(jnp.float32), (toks, 128)),
            cosine,
            sine,
        ),
        count,
        stages,
    )
    low = jnp.where(lax.axis_index("pipe") < stages - 1, low, jnp.zeros_like(low))
    return (kg[None], vg[None], low[None])


def solution(mesh):
    in_specs = (
        P("pipe", "dp", None),
        P("pipe", None),
        P("pipe", "dp", "tensor"),
        P("pipe", "dp", "tensor"),
        P("pipe", "dp", "tensor"),
        P("pipe", "dp", "tensor"),
        P("pipe", "dp"),
        P("pipe", "dp"),
        P("pipe", "dp"),
    )
    out_specs = (P("pipe", "dp", "tensor"), P("pipe", "dp", "tensor"), P("pipe", "dp", None))
    return jax.shard_map(
        on_device, mesh=mesh, in_specs=in_specs, out_specs=out_specs, check_vma=False
    )
```

```python
import functools
import math

import jax
import jax.numpy as jnp
from jax import lax
from jax.experimental import pallas as pl
from jax.experimental.pallas import tpu as pltpu
from jax.sharding import PartitionSpec as P

HD = 128


npo_beta = 0.1
norm_eps = 1e-05
rope_base = 500000.0


def rope_tables(length, head_dim):
    positions = jnp.arange(length).astype(jnp.float32)
    freq_index = jnp.arange(head_dim // 2).astype(jnp.float32)
    inverse = 1.0 / rope_base ** (2.0 * freq_index / head_dim)
    angles = positions[:, None] * inverse[None, :]
    cosine = jnp.concatenate([jnp.cos(angles), jnp.cos(angles)], axis=1)
    sine = jnp.concatenate([jnp.sin(angles), jnp.sin(angles)], axis=1)
    return (cosine, sine)


MESH = pl.DeviceIdType.MESH
VMEM_BYTES = 52 * 1024 * 1024


def remote(src, dst, send_sem, recv_sem, **where):
    return pltpu.make_async_remote_copy(
        src_ref=src, dst_ref=dst, send_sem=send_sem, recv_sem=recv_sem,
        device_id=where, device_id_type=MESH,
    )


def dot_nt(left, right):
    return lax.dot_general(
        left, right, (((1,), (1,)), ((), ())), preferred_element_type=jnp.float32
    )


def dot_tn(left, right):
    return lax.dot_general(
        left, right, (((0,), (0,)), ((), ())), preferred_element_type=jnp.float32
    )


FWD_CHUNKS = 4
BWD_CHUNKS = 8


def section_kernel(
    count, stages,
    hid, gain, kw, vw, query, cotan, factor, live, cosine, sine,
    low, kg_out, vg_out,
    wcat, normed, cols, total, psend, precv, woth, inv, raws,
    comb, cpart, pown, poth, ngs, ngr, cot, cother,
    zs, zr, ws, wr, fs, fr, ps, pr, ls,
    sa, ra, sb, rb, sc, rc, sn, rn, so, ro,
):
    p = lax.axis_index("pipe")
    z = lax.axis_index("dp")
    y = lax.axis_index("tensor")
    other = 1 - y
    toks, width = hid.shape
    rows = width // count
    half_rows = rows // 2
    kcols = kw.shape[1]
    heads = kcols // HD
    chunk = toks // BWD_CHUNKS
    half = toks // 2
    fchunk = half // FWD_CHUNKS
    has_lower = p > 0
    has_upper = p < stages - 1

    barrier = pltpu.get_barrier_semaphore()
    for d in range(1, count):
        pl.semaphore_signal(
            barrier, inc=1, device_id={"dp": lax.rem(z + d, count)}, device_id_type=MESH
        )
    pl.semaphore_signal(barrier, inc=1, device_id={"tensor": other}, device_id_type=MESH)

    @pl.when(has_lower)
    def _():
        pl.semaphore_signal(barrier, inc=1, device_id={"pipe": p - 1}, device_id_type=MESH)

    @pl.when(has_upper)
    def _():
        pl.semaphore_signal(barrier, inc=1, device_id={"pipe": p + 1}, device_id_type=MESH)

    for k in range(heads):
        head = pl.ds(k * HD, HD)
        wcat[:, pl.ds(2 * k * HD, HD)] = kw[:, head]
        wcat[:, pl.ds((2 * k + 1) * HD, HD)] = vw[:, head]
    peers = count + has_lower.astype(jnp.int32) + has_upper.astype(jnp.int32)
    pl.semaphore_wait(barrier, peers)

    def norm_half(which):
        def step(i, carry):
            at = pl.ds(pl.multiple_of(which * half + i * 16, 16), 16)
            h = hid[at, :].astype(jnp.float32)
            scale_row = lax.rsqrt(jnp.mean(h * h, axis=-1, keepdims=True) + norm_eps)
            normed[at, :] = (h * scale_row * gain[...]).astype(jnp.bfloat16)
            inv[at, :] = jnp.broadcast_to(scale_row, (16, 128))
            return carry

        lax.fori_loop(0, half // 16, step, 0)

    def rows_of(which, c):
        return pl.ds(pl.multiple_of(which * half + c * fchunk, 16), fchunk)

    norm_half(y)
    sent = []

    def column_copy(c, d):
        to = lax.rem(z + d, count)
        return remote(
            normed.at[rows_of(y, c), pl.ds(pl.multiple_of(to * rows, 128), rows)],
            cols.at[z, rows_of(y, c), :],
            zs.at[c, d - 1], zr.at[c, d - 1], dp=to,
        )

    for d in range(1, count):
        column_copy(0, d).start()
    give = pl.ds(pl.multiple_of(other * half_rows, 16), half_rows)
    wcopy = remote(wcat.at[give, :], woth, ws.at[0], wr.at[0], tensor=other)
    norm_half(other)
    own = pltpu.make_async_copy(
        normed.at[:, pl.ds(pl.multiple_of(z * rows, 128), rows)], cols.at[z], ls.at[0]
    )
    own.start()
    own.wait()

    step_k = min(rows, 512)

    def project(sources, c):
        def step(k, acc):
            at = pl.ds(pl.multiple_of(k * step_k, 128), step_k)
            parts = []
            for src in sources:
                parts.append(cols[src, pl.ds(c * fchunk, fchunk), at])
                parts.append(cols[src, pl.ds(half + c * fchunk, fchunk), at])
            a = jnp.concatenate(parts, axis=0)
            return acc + jnp.dot(a, wcat[at, :], preferred_element_type=jnp.float32)

        zero = jnp.zeros((len(sources) * 2 * fchunk, 2 * kcols), jnp.float32)
        return lax.fori_loop(0, rows // step_k, step, zero)

    for c in range(FWD_CHUNKS):
        if c == 1:
            for d in range(1, count):
                column_copy(0, d).wait_send()
                column_copy(1, d).start()
        total[c] = project([z], c)

    for c in range(FWD_CHUNKS):
        for d in range(1, count):
            src = lax.rem(z - d + count, count)
            place = cols.at[src, rows_of(y, c), :]
            remote(place, place, zs.at[c, d - 1], zr.at[c, d - 1], dp=src).wait_recv()
            copy = remote(place, place, fs.at[c, d - 1], fr.at[c, d - 1], tensor=other)
            copy.start()
            sent.append(copy)
        if c == FWD_CHUNKS - 1:
            wcopy.start()
        else:
            for d in range(1, count):
                column_copy(c + 1, d).wait_send()
                if c < FWD_CHUNKS - 2:
                    column_copy(c + 2, d).start()
        for first in range(1, count, 3):
            members = range(first, min(first + 3, count))
            sources = [lax.rem(z - d + count, count) for d in members]
            for d, src in zip(members, sources):
                place = cols.at[src, rows_of(other, c), :]
                remote(place, place, fs.at[c, d - 1], fr.at[c, d - 1], tensor=other).wait_recv()
            part = project(sources, c).astype(jnp.bfloat16)
            for i, d in enumerate(members):
                psend[d - 1, c] = part[i * 2 * fchunk : (i + 1) * 2 * fchunk]
                copy = remote(
                    psend.at[d - 1, c], precv.at[d - 1, c], ps.at[c, d - 1], pr.at[c, d - 1],
                    dp=sources[i],
                )
                copy.start()
                sent.append(copy)
    for c in range(FWD_CHUNKS):
        acc = total[c]
        for d in range(1, count):
            remote(
                psend.at[d - 1, c], precv.at[d - 1, c], ps.at[c, d - 1], pr.at[c, d - 1],
                dp=lax.rem(z + d, count),
            ).wait_recv()
            acc = acc + precv[d - 1, c].astype(jnp.float32)
        for which in range(2):
            raws[pl.ds(which * half + c * fchunk, fchunk), :] = acc[
                which * fchunk : (which + 1) * fchunk
            ]

    lane = lax.broadcasted_iota(jnp.int32, (toks, HD), 1)
    sign = jnp.where(lane < HD // 2, -1.0, 1.0)
    key_pos = lax.broadcasted_iota(jnp.int32, (toks, toks), 0)
    query_pos = lax.broadcasted_iota(jnp.int32, (toks, toks), 1)
    allowed = (key_pos <= query_pos) & (live[...][:, :1] > 0.0)
    bias = jnp.where(allowed, 0.0, -1e30)
    scale = 1.0 / math.sqrt(HD)
    group = query.shape[1] // kcols
    weigh = factor[...][:, :1]
    cen = jnp.zeros((toks, 1), jnp.float32)

    def pair(k):
        return pl.ds(2 * k * HD, 2 * HD)

    def piece_copy(d, k):
        return remote(
            comb.at[:, pair(k)], pown.at[z, :, pair(k)], sa.at[d - 1, k], ra.at[d - 1, k],
            dp=lax.rem(z + d, count),
        )

    for k in range(heads):
        raw = raws[:, pl.ds(2 * k * HD, HD)]
        val = raws[:, pl.ds((2 * k + 1) * HD, HD)]
        key = (raw * cosine[...] + pltpu.roll(raw, HD // 2, 1) * sign * sine[...]).astype(jnp.bfloat16)
        value = val.astype(jnp.bfloat16)
        vgrad = jnp.zeros((toks, HD), jnp.float32)
        rgrad = jnp.zeros((toks, HD), jnp.float32)
        for g in range(group):
            at = pl.ds((k * group + g) * HD, HD)
            q = query[:, at]
            co = (cotan[:, at].astype(jnp.float32) * weigh).astype(jnp.bfloat16)
            scores = dot_nt(key, q) * scale + bias
            expd = jnp.exp(scores - jnp.max(scores, axis=0, keepdims=True))
            probs = expd * (1.0 / jnp.sum(expd, axis=0, keepdims=True))
            pgrad = dot_nt(value, co)
            centre = jnp.sum(probs * pgrad, axis=0, keepdims=True)
            sgrad = (probs * (pgrad - centre) * scale).astype(jnp.bfloat16)
            vgrad = vgrad + jnp.dot(probs.astype(jnp.bfloat16), co, preferred_element_type=jnp.float32)
            rgrad = rgrad + jnp.dot(sgrad, q, preferred_element_type=jnp.float32)
        kgrad = rgrad * cosine[...] - pltpu.roll(rgrad * sine[...], HD // 2, 1) * sign
        klow, vlow = kgrad.astype(jnp.bfloat16), vgrad.astype(jnp.bfloat16)
        comb[:, pl.ds(2 * k * HD, HD)] = klow
        comb[:, pl.ds((2 * k + 1) * HD, HD)] = vlow
        cen = cen + jnp.sum(
            klow.astype(jnp.float32) * raw + vlow.astype(jnp.float32) * val,
            axis=1, keepdims=True,
        )
        for d in range(1, count):
            copy = piece_copy(d, k)
            copy.start()
            sent.append(copy)
        copy = remote(comb.at[:, pair(k)], poth.at[z, :, pair(k)], sb.at[0, k], rb.at[0, k], tensor=other)
        copy.start()
        sent.append(copy)
    cpart[...] = jnp.broadcast_to(cen, (toks, 128))
    ccopy = remote(cpart, cother, sc.at[0], rc.at[0], tensor=other)
    ccopy.start()
    pown[z] = comb[...]

    def cross_piece(d, k):
        place = lax.rem(z - d + count, count)
        return remote(
            pown.at[place, :, pair(k)], poth.at[place, :, pair(k)], sb.at[d, k], rb.at[d, k], tensor=other
        )

    for k in range(heads):
        for d in range(1, count):
            piece_copy(d, k).wait_recv()
            copy = cross_piece(d, k)
            copy.start()
            sent.append(copy)

    tile = min(half_rows, 256)

    def normed_grad(src, out, slot):
        def step(n, carry):
            mine = pl.ds(pl.multiple_of(y * half_rows + n * tile, 16), tile)
            at = pl.ds(pl.multiple_of(n * tile, 128), tile)
            a = dot_nt(pown[src], wcat[mine, :])
            b = dot_nt(poth[src], woth[at, :])
            both = a.astype(jnp.bfloat16).astype(jnp.float32) + b.astype(jnp.bfloat16).astype(jnp.float32)
            out[slot, :, at] = both.astype(jnp.bfloat16)
            return carry

        lax.fori_loop(0, half_rows // tile, step, 0)

    def wait_other(d):
        for k in range(heads):
            cross_piece(d, k).wait_recv()

    def grad_copy(c, d):
        at = pl.ds(c * chunk, chunk)
        return remote(
            ngs.at[d - 1, at, :], ngr.at[z, at, :], sn.at[c, d - 1], rn.at[c, d - 1],
            dp=lax.rem(z - d + count, count),
        )

    wcopy.wait()
    wait_other(0)
    normed_grad(z, ngr, z)
    for d in range(1, count):
        wait_other(d)
        normed_grad(lax.rem(z - d + count, count), ngs, d - 1)
        grad_copy(0, d).start()
    ccopy.wait()

    wtile = min(rows, 256)
    wsteps = rows // wtile

    def weight_grad(n, carry):
        at = pl.ds(pl.multiple_of(n * wtile, 128), wtile)
        acc = jnp.zeros((wtile, 2 * kcols), jnp.float32)
        for r in range(count):
            term = dot_tn(cols[r, :, at], pown[r])
            acc = acc + term.astype(jnp.bfloat16).astype(jnp.float32)
        low_acc = acc.astype(jnp.bfloat16)
        for k in range(heads):
            head = pl.ds(k * HD, HD)
            kg_out[at, head] = low_acc[:, 2 * k * HD : (2 * k + 1) * HD]
            vg_out[at, head] = low_acc[:, (2 * k + 1) * HD : (2 * k + 2) * HD]
        return carry

    def out_place(c, w, which):
        feat = pl.ds(pl.multiple_of(w * rows + which * half_rows, 128), half_rows)
        return low.at[pl.ds(c * chunk, chunk), feat]

    def out_copy(c, w, to):
        src = cot.at[w, pl.ds(c * chunk, chunk), :]
        return remote(src, out_place(c, w, y), so.at[c, w, 0], ro.at[c, w, 0], pipe=to)

    def cross_copy(c, w, which):
        place = out_place(c, w, which)
        return remote(place, place, so.at[c, w, 1], ro.at[c, w, 1], tensor=other)

    def pass_on(c):
        @pl.when(has_upper)
        def _():
            for w in range(count):
                out_copy(c, w, p + 1).wait_recv()
                cross_copy(c, w, y).start()

    for c in range(BWD_CHUNKS):
        for d in range(1, count):
            grad_copy(c, d).wait_send()
            if c < BWD_CHUNKS - 1:
                grad_copy(c + 1, d).start()
        for d in range(1, count):
            grad_copy(c, d).wait_recv()

        def tail(i, carry):
            at = pl.ds(pl.multiple_of(c * chunk + i * 16, 16), 16)
            inv_rms = inv[at, :][:, :1]
            centre = (cpart[at, :] + cother[at, :])[:, :1] * (1.0 / width)
            for w in range(count):
                feat = pl.ds(pl.multiple_of(w * rows + y * half_rows, 128), half_rows)
                nhat = hid[at, feat].astype(jnp.float32) * inv_rms
                grad_in = ngr[w, at, :].astype(jnp.float32) * gain[:, feat]
                cot[w, at, :] = ((grad_in - nhat * centre) * inv_rms).astype(jnp.bfloat16)
            return carry

        lax.fori_loop(0, chunk // 16, tail, 0)

        @pl.when(has_lower)
        def _():
            for w in range(count):
                out_copy(c, w, p - 1).start()

        lax.fori_loop(wsteps * c // BWD_CHUNKS, wsteps * (c + 1) // BWD_CHUNKS, weight_grad, 0)
        if c > 0:
            pass_on(c - 1)

    pass_on(BWD_CHUNKS - 1)

    for copy in sent:
        copy.wait_send()

    @pl.when(has_lower)
    def _():
        for c in range(BWD_CHUNKS):
            for w in range(count):
                out_copy(c, w, p - 1).wait_send()

    @pl.when(has_upper)
    def _():
        for c in range(BWD_CHUNKS):
            for w in range(count):
                cross_copy(c, w, y).wait_send()
                cross_copy(c, w, other).wait_recv()


def section_call(arrays, count, stages):
    hidden, _, kw = arrays[:3]
    toks, width = hidden.shape
    rows = width // count
    kcols = kw.shape[1]
    heads = kcols // HD
    low, wide = jnp.bfloat16, jnp.float32
    vmem = pl.BlockSpec(memory_space=pltpu.VMEM)
    hbm = pl.BlockSpec(memory_space=pl.ANY)
    dma = pltpu.SemaphoreType.DMA
    m = toks // FWD_CHUNKS
    fpair = (FWD_CHUNKS, count - 1)
    bpair = (BWD_CHUNKS, count - 1)
    trio = (BWD_CHUNKS, count, 2)
    others = count - 1
    return pl.pallas_call(
        functools.partial(section_kernel, count, stages),
        out_shape=(
            jax.ShapeDtypeStruct((toks, width), low),
            jax.ShapeDtypeStruct((rows, kcols), low),
            jax.ShapeDtypeStruct((rows, kcols), low),
        ),
        in_specs=[vmem] * 10,
        out_specs=(hbm, vmem, vmem),
        scratch_shapes=[
            pltpu.VMEM((rows, 2 * kcols), low),
            pltpu.VMEM((toks, width), low),
            pltpu.VMEM((count, toks, rows), low),
            pltpu.VMEM((FWD_CHUNKS, m, 2 * kcols), wide),
            pltpu.VMEM((others, FWD_CHUNKS, m, 2 * kcols), low),
            pltpu.VMEM((others, FWD_CHUNKS, m, 2 * kcols), low),
            pltpu.VMEM((rows // 2, 2 * kcols), low),
            pltpu.VMEM((toks, 128), wide),
            pltpu.VMEM((toks, 2 * kcols), wide),
            pltpu.VMEM((toks, 2 * kcols), low),
            pltpu.VMEM((toks, 128), wide),
            pltpu.VMEM((count, toks, 2 * kcols), low),
            pltpu.VMEM((count, toks, 2 * kcols), low),
            pltpu.VMEM((others, toks, rows // 2), low),
            pltpu.VMEM((count, toks, rows // 2), low),
            pltpu.VMEM((count, toks, rows // 2), low),
            pltpu.VMEM((toks, 128), wide),
            dma(fpair), dma(fpair), dma((1,)), dma((1,)), dma(fpair), dma(fpair), dma(fpair), dma(fpair),
            dma((1,)),
            dma((others, heads)), dma((others, heads)), dma((count, heads)), dma((count, heads)), dma((1,)), dma((1,)),
            dma(bpair), dma(bpair), dma(trio), dma(trio),
        ],
        compiler_params=pltpu.CompilerParams(
            collective_id=0, has_side_effects=True, vmem_limit_bytes=VMEM_BYTES
        ),
        name="section",
    )(*arrays)


def on_device(
    hidden_states,
    norm_gain,
    key_weight,
    value_weight,
    queries,
    context_cotangent,
    lengths,
    policy_logp,
    reference_logp,
):
    count = lax.axis_size("dp")
    stages = lax.axis_size("pipe")
    hidden = hidden_states[0]
    toks = hidden.shape[0]
    assert lengths.shape[1] == 1 and lax.axis_size("tensor") == 2
    cosine, sine = rope_tables(toks, HD)
    seq_weight = 2.0 * jax.nn.sigmoid(npo_beta * (policy_logp[0] - reference_logp[0])) / count
    live = jnp.arange(toks)[:, None] < lengths[0][None, :]
    factor = jnp.where(live, seq_weight[None, :], 0.0)
    low, kg, vg = section_call(
        (
            hidden,
            norm_gain.astype(jnp.float32),
            key_weight[0],
            value_weight[0],
            queries[0],
            context_cotangent[0],
            jnp.broadcast_to(factor, (toks, 128)),
            jnp.broadcast_to(live.astype(jnp.float32), (toks, 128)),
            cosine,
            sine,
        ),
        count,
        stages,
    )
    low = jnp.where(lax.axis_index("pipe") < stages - 1, low, jnp.zeros_like(low))
    return (kg[None], vg[None], low[None])


def solution(mesh):
    in_specs = (
        P("pipe", "dp", None),
        P("pipe", None),
        P("pipe", "dp", "tensor"),
        P("pipe", "dp", "tensor"),
        P("pipe", "dp", "tensor"),
        P("pipe", "dp", "tensor"),
        P("pipe", "dp"),
        P("pipe", "dp"),
        P("pipe", "dp"),
    )
    out_specs = (P("pipe", "dp", "tensor"), P("pipe", "dp", "tensor"), P("pipe", "dp", None))
    return jax.shard_map(
        on_device, mesh=mesh, in_specs=in_specs, out_specs=out_specs, check_vma=False
    )
```

```python
import functools
import math

import jax
import jax.numpy as jnp
from jax import lax
from jax.experimental import pallas as pl
from jax.experimental.pallas import tpu as pltpu
from jax.sharding import PartitionSpec as P

HD = 128


npo_beta = 0.1
norm_eps = 1e-05
rope_base = 500000.0


def rope_tables(length, head_dim):
    positions = jnp.arange(length).astype(jnp.float32)
    freq_index = jnp.arange(head_dim // 2).astype(jnp.float32)
    inverse = 1.0 / rope_base ** (2.0 * freq_index / head_dim)
    angles = positions[:, None] * inverse[None, :]
    cosine = jnp.concatenate([jnp.cos(angles), jnp.cos(angles)], axis=1)
    sine = jnp.concatenate([jnp.sin(angles), jnp.sin(angles)], axis=1)
    return (cosine, sine)


MESH = pl.DeviceIdType.MESH
VMEM_BYTES = 52 * 1024 * 1024


def remote(src, dst, send_sem, recv_sem, **where):
    return pltpu.make_async_remote_copy(
        src_ref=src, dst_ref=dst, send_sem=send_sem, recv_sem=recv_sem,
        device_id=where, device_id_type=MESH,
    )


def dot_nt(left, right):
    return lax.dot_general(
        left, right, (((1,), (1,)), ((), ())), preferred_element_type=jnp.float32
    )


def dot_tn(left, right):
    return lax.dot_general(
        left, right, (((0,), (0,)), ((), ())), preferred_element_type=jnp.float32
    )


FWD_CHUNKS = 4
BWD_CHUNKS = 8


def section_kernel(
    count, stages,
    hid, gain, kw, vw, query, cotan, factor, live, cosine, sine,
    low, kg_out, vg_out,
    wcat, normed, cols, total, psend, precv, woth, inv, raws,
    comb, cpart, pown, poth, ngs, ngr, cot, cother, stage,
    zs, zr, ws, wr, fs, fr, ps, pr, ls,
    sa, ra, sb, rb, sc, rc, sn, rn, so, ro, sg, rg, sh,
):
    p = lax.axis_index("pipe")
    z = lax.axis_index("dp")
    y = lax.axis_index("tensor")
    other = 1 - y
    toks, width = hid.shape
    rows = width // count
    half_rows = rows // 2
    kcols = kw.shape[1]
    heads = kcols // HD
    chunk = toks // BWD_CHUNKS
    half = toks // 2
    fchunk = half // FWD_CHUNKS
    has_lower = p > 0
    has_upper = p < stages - 1

    barrier = pltpu.get_barrier_semaphore()
    for d in range(1, count):
        pl.semaphore_signal(
            barrier, inc=1, device_id={"dp": lax.rem(z + d, count)}, device_id_type=MESH
        )
    pl.semaphore_signal(barrier, inc=1, device_id={"tensor": other}, device_id_type=MESH)

    @pl.when(has_lower)
    def _():
        pl.semaphore_signal(barrier, inc=1, device_id={"pipe": p - 1}, device_id_type=MESH)

    @pl.when(has_upper)
    def _():
        pl.semaphore_signal(barrier, inc=1, device_id={"pipe": p + 1}, device_id_type=MESH)

    for k in range(heads):
        head = pl.ds(k * HD, HD)
        wcat[:, pl.ds(2 * k * HD, HD)] = kw[:, head]
        wcat[:, pl.ds((2 * k + 1) * HD, HD)] = vw[:, head]
    peers = count + has_lower.astype(jnp.int32) + has_upper.astype(jnp.int32)
    pl.semaphore_wait(barrier, peers)

    def norm_rows(which, first, last):
        def step(i, carry):
            at = pl.ds(pl.multiple_of(which * half + i * 16, 16), 16)
            h = hid[at, :].astype(jnp.float32)
            scale_row = lax.rsqrt(jnp.mean(h * h, axis=-1, keepdims=True) + norm_eps)
            normed[at, :] = (h * scale_row * gain[...]).astype(jnp.bfloat16)
            inv[at, :] = jnp.broadcast_to(scale_row, (16, 128))
            return carry

        lax.fori_loop(first // 16, last // 16, step, 0)

    def rows_of(which, c):
        return pl.ds(pl.multiple_of(which * half + c * fchunk, 16), fchunk)

    norm_rows(y, 0, fchunk)
    sent = []

    def column_copy(c, d):
        to = lax.rem(z + d, count)
        return remote(
            normed.at[rows_of(y, c), pl.ds(pl.multiple_of(to * rows, 128), rows)],
            cols.at[z, rows_of(y, c), :],
            zs.at[c, d - 1], zr.at[c, d - 1], dp=to,
        )

    for d in range(1, count):
        column_copy(0, d).start()
    give = pl.ds(pl.multiple_of(other * half_rows, 16), half_rows)
    wcopy = remote(wcat.at[give, :], woth, ws.at[0], wr.at[0], tensor=other)
    norm_rows(y, fchunk, half)
    norm_rows(other, 0, half)
    own = pltpu.make_async_copy(
        normed.at[:, pl.ds(pl.multiple_of(z * rows, 128), rows)], cols.at[z], ls.at[0]
    )
    own.start()
    own.wait()

    step_k = min(rows, 512)

    def project(sources, c):
        def step(k, acc):
            at = pl.ds(pl.multiple_of(k * step_k, 128), step_k)
            parts = []
            for src in sources:
                parts.append(cols[src, pl.ds(c * fchunk, fchunk), at])
                parts.append(cols[src, pl.ds(half + c * fchunk, fchunk), at])
            a = jnp.concatenate(parts, axis=0)
            return acc + jnp.dot(a, wcat[at, :], preferred_element_type=jnp.float32)

        zero = jnp.zeros((len(sources) * 2 * fchunk, 2 * kcols), jnp.float32)
        return lax.fori_loop(0, rows // step_k, step, zero)

    for c in range(FWD_CHUNKS):
        if c == 1:
            for d in range(1, count):
                column_copy(0, d).wait_send()
                column_copy(1, d).start()
        total[c] = project([z], c)

    for c in range(FWD_CHUNKS):
        for d in range(1, count):
            src = lax.rem(z - d + count, count)
            place = cols.at[src, rows_of(y, c), :]
            remote(place, place, zs.at[c, d - 1], zr.at[c, d - 1], dp=src).wait_recv()
            copy = remote(place, place, fs.at[c, d - 1], fr.at[c, d - 1], tensor=other)
            copy.start()
            sent.append(copy)
        if c == FWD_CHUNKS - 1:
            wcopy.start()
        else:
            for d in range(1, count):
                column_copy(c + 1, d).wait_send()
                if c < FWD_CHUNKS - 2:
                    column_copy(c + 2, d).start()
        for first in range(1, count, 3):
            members = range(first, min(first + 3, count))
            sources = [lax.rem(z - d + count, count) for d in members]
            for d, src in zip(members, sources):
                place = cols.at[src, rows_of(other, c), :]
                remote(place, place, fs.at[c, d - 1], fr.at[c, d - 1], tensor=other).wait_recv()
            part = project(sources, c).astype(jnp.bfloat16)
            for i, d in enumerate(members):
                psend[d - 1, c] = part[i * 2 * fchunk : (i + 1) * 2 * fchunk]
                copy = remote(
                    psend.at[d - 1, c], precv.at[d - 1, c], ps.at[c, d - 1], pr.at[c, d - 1],
                    dp=sources[i],
                )
                copy.start()
                sent.append(copy)
    for c in range(FWD_CHUNKS):
        acc = total[c]
        for d in range(1, count):
            remote(
                psend.at[d - 1, c], precv.at[d - 1, c], ps.at[c, d - 1], pr.at[c, d - 1],
                dp=lax.rem(z + d, count),
            ).wait_recv()
            acc = acc + precv[d - 1, c].astype(jnp.float32)
        for which in range(2):
            raws[pl.ds(which * half + c * fchunk, fchunk), :] = acc[
                which * fchunk : (which + 1) * fchunk
            ]

    lane = lax.broadcasted_iota(jnp.int32, (toks, HD), 1)
    sign = jnp.where(lane < HD // 2, -1.0, 1.0)
    key_pos = lax.broadcasted_iota(jnp.int32, (toks, toks), 0)
    query_pos = lax.broadcasted_iota(jnp.int32, (toks, toks), 1)
    allowed = (key_pos <= query_pos) & (live[...][:, :1] > 0.0)
    bias = jnp.where(allowed, 0.0, -1e30)
    scale = 1.0 / math.sqrt(HD)
    group = query.shape[1] // kcols
    weigh = factor[...][:, :1]
    cen = jnp.zeros((toks, 1), jnp.float32)

    def pair(k):
        return pl.ds(2 * k * HD, 2 * HD)

    def piece_copy(d, k):
        return remote(
            comb.at[:, pair(k)], pown.at[z, :, pair(k)], sa.at[d - 1, k], ra.at[d - 1, k],
            dp=lax.rem(z + d, count),
        )

    for k in range(heads):
        raw = raws[:, pl.ds(2 * k * HD, HD)]
        val = raws[:, pl.ds((2 * k + 1) * HD, HD)]
        key = (raw * cosine[...] + pltpu.roll(raw, HD // 2, 1) * sign * sine[...]).astype(jnp.bfloat16)
        value = val.astype(jnp.bfloat16)
        vgrad = jnp.zeros((toks, HD), jnp.float32)
        rgrad = jnp.zeros((toks, HD), jnp.float32)
        for g in range(group):
            at = pl.ds((k * group + g) * HD, HD)
            q = query[:, at]
            co = (cotan[:, at].astype(jnp.float32) * weigh).astype(jnp.bfloat16)
            scores = dot_nt(key, q) * scale + bias
            expd = jnp.exp(scores - jnp.max(scores, axis=0, keepdims=True))
            probs = expd * (1.0 / jnp.sum(expd, axis=0, keepdims=True))
            pgrad = dot_nt(value, co)
            centre = jnp.sum(probs * pgrad, axis=0, keepdims=True)
            sgrad = (probs * (pgrad - centre) * scale).astype(jnp.bfloat16)
            vgrad = vgrad + jnp.dot(probs.astype(jnp.bfloat16), co, preferred_element_type=jnp.float32)
            rgrad = rgrad + jnp.dot(sgrad, q, preferred_element_type=jnp.float32)
        kgrad = rgrad * cosine[...] - pltpu.roll(rgrad * sine[...], HD // 2, 1) * sign
        klow, vlow = kgrad.astype(jnp.bfloat16), vgrad.astype(jnp.bfloat16)
        comb[:, pl.ds(2 * k * HD, HD)] = klow
        comb[:, pl.ds((2 * k + 1) * HD, HD)] = vlow
        cen = cen + jnp.sum(
            klow.astype(jnp.float32) * raw + vlow.astype(jnp.float32) * val,
            axis=1, keepdims=True,
        )
        for d in range(1, count):
            copy = piece_copy(d, k)
            copy.start()
            sent.append(copy)
        copy = remote(comb.at[:, pair(k)], poth.at[z, :, pair(k)], sb.at[0, k], rb.at[0, k], tensor=other)
        copy.start()
        sent.append(copy)
    cpart[...] = jnp.broadcast_to(cen, (toks, 128))
    ccopy = remote(cpart, cother, sc.at[0], rc.at[0], tensor=other)
    ccopy.start()
    pown[z] = comb[...]

    def cross_piece(d, k):
        place = lax.rem(z - d + count, count)
        return remote(
            pown.at[place, :, pair(k)], poth.at[place, :, pair(k)], sb.at[d, k], rb.at[d, k], tensor=other
        )

    for k in range(heads):
        for d in range(1, count):
            piece_copy(d, k).wait_recv()
            copy = cross_piece(d, k)
            copy.start()
            sent.append(copy)

    tile = min(half_rows, 256)

    def normed_grad(src, out, slot):
        def step(n, carry):
            mine = pl.ds(pl.multiple_of(y * half_rows + n * tile, 16), tile)
            at = pl.ds(pl.multiple_of(n * tile, 128), tile)
            a = dot_nt(pown[src], wcat[mine, :])
            b = dot_nt(poth[src], woth[at, :])
            both = a.astype(jnp.bfloat16).astype(jnp.float32) + b.astype(jnp.bfloat16).astype(jnp.float32)
            out[slot, :, at] = both.astype(jnp.bfloat16)
            return carry

        lax.fori_loop(0, half_rows // tile, step, 0)

    def wait_other(d):
        for k in range(heads):
            cross_piece(d, k).wait_recv()

    def grad_copy(c, d):
        at = pl.ds(c * chunk, chunk)
        return remote(
            ngs.at[d - 1, at, :], ngr.at[z, at, :], sn.at[c, d - 1], rn.at[c, d - 1],
            dp=lax.rem(z - d + count, count),
        )

    wcopy.wait()
    wait_other(0)
    normed_grad(z, ngr, z)
    for d in range(1, count):
        wait_other(d)
        normed_grad(lax.rem(z - d + count, count), ngs, d - 1)
        grad_copy(0, d).start()
    for d in range(1, count):
        grad_copy(1, d).start()
    ccopy.wait()

    wtile = min(rows, 256)
    wsteps = rows // wtile

    def weight_grad(n, carry):
        at = pl.ds(pl.multiple_of(n * wtile, 128), wtile)
        acc = jnp.zeros((wtile, 2 * kcols), jnp.float32)
        for r in range(count):
            term = dot_tn(cols[r, :, at], pown[r])
            acc = acc + term.astype(jnp.bfloat16).astype(jnp.float32)
        low_acc = acc.astype(jnp.bfloat16)
        for k in range(heads):
            head = pl.ds(k * HD, HD)
            kg_out[at, head] = low_acc[:, 2 * k * HD : (2 * k + 1) * HD]
            vg_out[at, head] = low_acc[:, (2 * k + 1) * HD : (2 * k + 2) * HD]
        return carry

    def out_place(c, w, which):
        feat = pl.ds(pl.multiple_of(w * rows + which * half_rows, 128), half_rows)
        return low.at[pl.ds(c * chunk, chunk), feat]

    def out_copy(c, w, to):
        src = cot.at[w, pl.ds(c * chunk, chunk), :]
        return remote(src, out_place(c, w, y), so.at[c, w, 0], ro.at[c, w, 0], pipe=to)

    def cross_copy(c, w, which):
        place = out_place(c, w, which)
        return remote(place, place, so.at[c, w, 1], ro.at[c, w, 1], tensor=other)

    first_staged = count // 2
    staging = has_lower & (lax.rem(p, 2) == 0)
    passes_all = has_upper & (lax.rem(p, 2) == 0)

    def stage_copy(c, w):
        at = pl.ds(c * chunk, chunk)
        i = w - first_staged
        return remote(
            cot.at[w, at, :], stage.at[i, at, :], sg.at[c, i], rg.at[c, i], tensor=other
        )

    def staged_out(c, w):
        i = w - first_staged
        return remote(
            stage.at[i, pl.ds(c * chunk, chunk), :], out_place(c, w, other),
            sh.at[c, i], ro.at[c, w, 1], pipe=p - 1,
        )

    def pass_on(c):
        @pl.when(staging)
        def _():
            for w in range(first_staged, count):
                stage_copy(c, w).wait_recv()
                staged_out(c, w).start()

        @pl.when(has_upper)
        def _():
            for w in range(count):
                out_copy(c, w, p + 1).wait_recv()
                if w < first_staged:
                    cross_copy(c, w, y).start()

        @pl.when(passes_all)
        def _():
            for w in range(first_staged, count):
                cross_copy(c, w, y).start()

    for c in range(BWD_CHUNKS):
        for d in range(1, count):
            grad_copy(c, d).wait_send()
            if c < BWD_CHUNKS - 2:
                grad_copy(c + 2, d).start()
        for d in range(1, count):
            grad_copy(c, d).wait_recv()

        def tail(i, carry):
            at = pl.ds(pl.multiple_of(c * chunk + i * 16, 16), 16)
            inv_rms = inv[at, :][:, :1]
            centre = (cpart[at, :] + cother[at, :])[:, :1] * (1.0 / width)
            for w in range(count):
                feat = pl.ds(pl.multiple_of(w * rows + y * half_rows, 128), half_rows)
                nhat = hid[at, feat].astype(jnp.float32) * inv_rms
                grad_in = ngr[w, at, :].astype(jnp.float32) * gain[:, feat]
                cot[w, at, :] = ((grad_in - nhat * centre) * inv_rms).astype(jnp.bfloat16)
            return carry

        lax.fori_loop(0, chunk // 16, tail, 0)

        @pl.when(has_lower)
        def _():
            for w in range(count):
                out_copy(c, w, p - 1).start()

        @pl.when(staging)
        def _():
            for w in range(first_staged, count):
                stage_copy(c, w).start()

        lax.fori_loop(wsteps * c // BWD_CHUNKS, wsteps * (c + 1) // BWD_CHUNKS, weight_grad, 0)
        if c > 0:
            pass_on(c - 1)

    pass_on(BWD_CHUNKS - 1)

    for copy in sent:
        copy.wait_send()

    @pl.when(has_lower)
    def _():
        for c in range(BWD_CHUNKS):
            for w in range(count):
                out_copy(c, w, p - 1).wait_send()

    @pl.when(has_upper)
    def _():
        for c in range(BWD_CHUNKS):
            for w in range(count):
                if w < first_staged:
                    cross_copy(c, w, y).wait_send()
                cross_copy(c, w, other).wait_recv()

    @pl.when(passes_all)
    def _():
        for c in range(BWD_CHUNKS):
            for w in range(first_staged, count):
                cross_copy(c, w, y).wait_send()

    @pl.when(staging)
    def _():
        for c in range(BWD_CHUNKS):
            for w in range(first_staged, count):
                stage_copy(c, w).wait_send()
                staged_out(c, w).wait_send()


def section_call(arrays, count, stages):
    hidden, _, kw = arrays[:3]
    toks, width = hidden.shape
    rows = width // count
    kcols = kw.shape[1]
    heads = kcols // HD
    low, wide = jnp.bfloat16, jnp.float32
    vmem = pl.BlockSpec(memory_space=pltpu.VMEM)
    hbm = pl.BlockSpec(memory_space=pl.ANY)
    dma = pltpu.SemaphoreType.DMA
    m = toks // FWD_CHUNKS
    fpair = (FWD_CHUNKS, count - 1)
    bpair = (BWD_CHUNKS, count - 1)
    trio = (BWD_CHUNKS, count, 2)
    staged = (BWD_CHUNKS, count - count // 2)
    others = count - 1
    return pl.pallas_call(
        functools.partial(section_kernel, count, stages),
        out_shape=(
            jax.ShapeDtypeStruct((toks, width), low),
            jax.ShapeDtypeStruct((rows, kcols), low),
            jax.ShapeDtypeStruct((rows, kcols), low),
        ),
        in_specs=[vmem] * 10,
        out_specs=(hbm, vmem, vmem),
        scratch_shapes=[
            pltpu.VMEM((rows, 2 * kcols), low),
            pltpu.VMEM((toks, width), low),
            pltpu.VMEM((count, toks, rows), low),
            pltpu.VMEM((FWD_CHUNKS, m, 2 * kcols), wide),
            pltpu.VMEM((others, FWD_CHUNKS, m, 2 * kcols), low),
            pltpu.VMEM((others, FWD_CHUNKS, m, 2 * kcols), low),
            pltpu.VMEM((rows // 2, 2 * kcols), low),
            pltpu.VMEM((toks, 128), wide),
            pltpu.VMEM((toks, 2 * kcols), wide),
            pltpu.VMEM((toks, 2 * kcols), low),
            pltpu.VMEM((toks, 128), wide),
            pltpu.VMEM((count, toks, 2 * kcols), low),
            pltpu.VMEM((count, toks, 2 * kcols), low),
            pltpu.VMEM((others, toks, rows // 2), low),
            pltpu.VMEM((count, toks, rows // 2), low),
            pltpu.VMEM((count, toks, rows // 2), low),
            pltpu.VMEM((toks, 128), wide),
            pltpu.VMEM((count - count // 2, toks, rows // 2), low),
            dma(fpair), dma(fpair), dma((1,)), dma((1,)), dma(fpair), dma(fpair), dma(fpair), dma(fpair),
            dma((1,)),
            dma((others, heads)), dma((others, heads)), dma((count, heads)), dma((count, heads)), dma((1,)), dma((1,)),
            dma(bpair), dma(bpair), dma(trio), dma(trio), dma(staged), dma(staged), dma(staged),
        ],
        compiler_params=pltpu.CompilerParams(
            collective_id=0, has_side_effects=True, vmem_limit_bytes=VMEM_BYTES
        ),
        name="section",
    )(*arrays)


def on_device(
    hidden_states,
    norm_gain,
    key_weight,
    value_weight,
    queries,
    context_cotangent,
    lengths,
    policy_logp,
    reference_logp,
):
    count = lax.axis_size("dp")
    stages = lax.axis_size("pipe")
    hidden = hidden_states[0]
    toks = hidden.shape[0]
    assert lengths.shape[1] == 1 and lax.axis_size("tensor") == 2
    cosine, sine = rope_tables(toks, HD)
    seq_weight = 2.0 * jax.nn.sigmoid(npo_beta * (policy_logp[0] - reference_logp[0])) / count
    live = jnp.arange(toks)[:, None] < lengths[0][None, :]
    factor = jnp.where(live, seq_weight[None, :], 0.0)
    low, kg, vg = section_call(
        (
            hidden,
            norm_gain.astype(jnp.float32),
            key_weight[0],
            value_weight[0],
            queries[0],
            context_cotangent[0],
            jnp.broadcast_to(factor, (toks, 128)),
            jnp.broadcast_to(live.astype(jnp.float32), (toks, 128)),
            cosine,
            sine,
        ),
        count,
        stages,
    )
    low = jnp.where(lax.axis_index("pipe") < stages - 1, low, jnp.zeros_like(low))
    return (kg[None], vg[None], low[None])


def solution(mesh):
    in_specs = (
        P("pipe", "dp", None),
        P("pipe", None),
        P("pipe", "dp", "tensor"),
        P("pipe", "dp", "tensor"),
        P("pipe", "dp", "tensor"),
        P("pipe", "dp", "tensor"),
        P("pipe", "dp"),
        P("pipe", "dp"),
        P("pipe", "dp"),
    )
    out_specs = (P("pipe", "dp", "tensor"), P("pipe", "dp", "tensor"), P("pipe", "dp", None))
    return jax.shard_map(
        on_device, mesh=mesh, in_specs=in_specs, out_specs=out_specs, check_vma=False
    )
```

```python
import functools
import math

import jax
import jax.numpy as jnp
from jax import lax
from jax.experimental import pallas as pl
from jax.experimental.pallas import tpu as pltpu
from jax.sharding import PartitionSpec as P

HD = 128


npo_beta = 0.1
norm_eps = 1e-05
rope_base = 500000.0


def rope_tables(length, head_dim):
    positions = jnp.arange(length).astype(jnp.float32)
    freq_index = jnp.arange(head_dim // 2).astype(jnp.float32)
    inverse = 1.0 / rope_base ** (2.0 * freq_index / head_dim)
    angles = positions[:, None] * inverse[None, :]
    cosine = jnp.concatenate([jnp.cos(angles), jnp.cos(angles)], axis=1)
    sine = jnp.concatenate([jnp.sin(angles), jnp.sin(angles)], axis=1)
    return (cosine, sine)


MESH = pl.DeviceIdType.MESH
VMEM_BYTES = 52 * 1024 * 1024


def remote(src, dst, send_sem, recv_sem, **where):
    return pltpu.make_async_remote_copy(
        src_ref=src, dst_ref=dst, send_sem=send_sem, recv_sem=recv_sem,
        device_id=where, device_id_type=MESH,
    )


def dot_nt(left, right):
    return lax.dot_general(
        left, right, (((1,), (1,)), ((), ())), preferred_element_type=jnp.float32
    )


def dot_tn(left, right):
    return lax.dot_general(
        left, right, (((0,), (0,)), ((), ())), preferred_element_type=jnp.float32
    )


FWD_CHUNKS = 4
BWD_CHUNKS = 8


def section_kernel(
    count, stages,
    hid, gain, kw, vw, query, cotan, factor, live, cosine, sine,
    low, kg_out, vg_out,
    wcat, normed, cols, total, psend, precv, woth, inv, raws,
    comb, cpart, pown, poth, ngs, ngr, cot, cother, stage,
    zs, zr, ws, wr, fs, fr, ps, pr, ls,
    sa, ra, sb, rb, sc, rc, sn, rn, so, ro, sg, rg, sh,
):
    p = lax.axis_index("pipe")
    z = lax.axis_index("dp")
    y = lax.axis_index("tensor")
    other = 1 - y
    toks, width = hid.shape
    rows = width // count
    half_rows = rows // 2
    kcols = kw.shape[1]
    heads = kcols // HD
    chunk = toks // BWD_CHUNKS
    half = toks // 2
    fchunk = half // FWD_CHUNKS
    has_lower = p > 0
    has_upper = p < stages - 1

    barrier = pltpu.get_barrier_semaphore()
    for d in range(1, count):
        pl.semaphore_signal(
            barrier, inc=1, device_id={"dp": lax.rem(z + d, count)}, device_id_type=MESH
        )
    pl.semaphore_signal(barrier, inc=1, device_id={"tensor": other}, device_id_type=MESH)

    @pl.when(has_lower)
    def _():
        pl.semaphore_signal(barrier, inc=1, device_id={"pipe": p - 1}, device_id_type=MESH)

    @pl.when(has_upper)
    def _():
        pl.semaphore_signal(barrier, inc=1, device_id={"pipe": p + 1}, device_id_type=MESH)

    for k in range(heads):
        head = pl.ds(k * HD, HD)
        wcat[:, pl.ds(2 * k * HD, HD)] = kw[:, head]
        wcat[:, pl.ds((2 * k + 1) * HD, HD)] = vw[:, head]
    peers = count + has_lower.astype(jnp.int32) + has_upper.astype(jnp.int32)
    pl.semaphore_wait(barrier, peers)

    def norm_rows(which, first, last):
        def step(i, carry):
            at = pl.ds(pl.multiple_of(which * half + i * 16, 16), 16)
            h = hid[at, :].astype(jnp.float32)
            scale_row = lax.rsqrt(jnp.mean(h * h, axis=-1, keepdims=True) + norm_eps)
            normed[at, :] = (h * scale_row * gain[...]).astype(jnp.bfloat16)
            inv[at, :] = jnp.broadcast_to(scale_row, (16, 128))
            return carry

        lax.fori_loop(first // 16, last // 16, step, 0)

    def rows_of(which, c):
        return pl.ds(pl.multiple_of(which * half + c * fchunk, 16), fchunk)

    norm_rows(y, 0, fchunk)
    sent = []

    def column_copy(c, d):
        to = lax.rem(z + d, count)
        return remote(
            normed.at[rows_of(y, c), pl.ds(pl.multiple_of(to * rows, 128), rows)],
            cols.at[z, rows_of(y, c), :],
            zs.at[c, d - 1], zr.at[c, d - 1], dp=to,
        )

    for d in range(1, count):
        column_copy(0, d).start()
    give = pl.ds(pl.multiple_of(other * half_rows, 16), half_rows)
    wcopy = remote(wcat.at[give, :], woth, ws.at[0], wr.at[0], tensor=other)
    norm_rows(y, fchunk, half)
    norm_rows(other, 0, half)
    own = pltpu.make_async_copy(
        normed.at[:, pl.ds(pl.multiple_of(z * rows, 128), rows)], cols.at[z], ls.at[0]
    )
    own.start()
    own.wait()

    step_k = min(rows, 512)

    def project(sources, c):
        def step(k, acc):
            at = pl.ds(pl.multiple_of(k * step_k, 128), step_k)
            parts = []
            for src in sources:
                parts.append(cols[src, pl.ds(c * fchunk, fchunk), at])
                parts.append(cols[src, pl.ds(half + c * fchunk, fchunk), at])
            a = jnp.concatenate(parts, axis=0)
            return acc + jnp.dot(a, wcat[at, :], preferred_element_type=jnp.float32)

        zero = jnp.zeros((len(sources) * 2 * fchunk, 2 * kcols), jnp.float32)
        return lax.fori_loop(0, rows // step_k, step, zero)

    for c in range(FWD_CHUNKS):
        if c == 1:
            for d in range(1, count):
                column_copy(0, d).wait_send()
                column_copy(1, d).start()
        total[c] = project([z], c)

    for c in range(FWD_CHUNKS):
        for d in range(1, count):
            src = lax.rem(z - d + count, count)
            place = cols.at[src, rows_of(y, c), :]
            remote(place, place, zs.at[c, d - 1], zr.at[c, d - 1], dp=src).wait_recv()
            copy = remote(place, place, fs.at[c, d - 1], fr.at[c, d - 1], tensor=other)
            copy.start()
            sent.append(copy)
        if c == FWD_CHUNKS - 1:
            wcopy.start()
        else:
            for d in range(1, count):
                column_copy(c + 1, d).wait_send()
                if c < FWD_CHUNKS - 2:
                    column_copy(c + 2, d).start()
        for first in range(1, count, 3):
            members = range(first, min(first + 3, count))
            sources = [lax.rem(z - d + count, count) for d in members]
            for d, src in zip(members, sources):
                place = cols.at[src, rows_of(other, c), :]
                remote(place, place, fs.at[c, d - 1], fr.at[c, d - 1], tensor=other).wait_recv()
            part = project(sources, c).astype(jnp.bfloat16)
            for i, d in enumerate(members):
                psend[d - 1, c] = part[i * 2 * fchunk : (i + 1) * 2 * fchunk]
                copy = remote(
                    psend.at[d - 1, c], precv.at[d - 1, c], ps.at[c, d - 1], pr.at[c, d - 1],
                    dp=sources[i],
                )
                copy.start()
                sent.append(copy)
    for c in range(FWD_CHUNKS):
        acc = total[c]
        for d in range(1, count):
            remote(
                psend.at[d - 1, c], precv.at[d - 1, c], ps.at[c, d - 1], pr.at[c, d - 1],
                dp=lax.rem(z + d, count),
            ).wait_recv()
            acc = acc + precv[d - 1, c].astype(jnp.float32)
        for which in range(2):
            raws[pl.ds(which * half + c * fchunk, fchunk), :] = acc[
                which * fchunk : (which + 1) * fchunk
            ]

    lane = lax.broadcasted_iota(jnp.int32, (toks, HD), 1)
    sign = jnp.where(lane < HD // 2, -1.0, 1.0)
    key_pos = lax.broadcasted_iota(jnp.int32, (toks, toks), 0)
    query_pos = lax.broadcasted_iota(jnp.int32, (toks, toks), 1)
    allowed = (key_pos <= query_pos) & (live[...][:, :1] > 0.0)
    bias = jnp.where(allowed, 0.0, -1e30)
    scale = 1.0 / math.sqrt(HD)
    group = query.shape[1] // kcols
    weigh = factor[...][:, :1]
    cen = jnp.zeros((toks, 1), jnp.float32)

    def pair(k):
        return pl.ds(2 * k * HD, 2 * HD)

    def piece_copy(d, k):
        return remote(
            comb.at[:, pair(k)], pown.at[z, :, pair(k)], sa.at[d - 1, k], ra.at[d - 1, k],
            dp=lax.rem(z + d, count),
        )

    for k in range(heads):
        raw = raws[:, pl.ds(2 * k * HD, HD)]
        val = raws[:, pl.ds((2 * k + 1) * HD, HD)]
        key = (raw * cosine[...] + pltpu.roll(raw, HD // 2, 1) * sign * sine[...]).astype(jnp.bfloat16)
        value = val.astype(jnp.bfloat16)
        vgrad = jnp.zeros((toks, HD), jnp.float32)
        rgrad = jnp.zeros((toks, HD), jnp.float32)
        for g in range(group):
            at = pl.ds((k * group + g) * HD, HD)
            q = query[:, at]
            co = (cotan[:, at].astype(jnp.float32) * weigh).astype(jnp.bfloat16)
            scores = dot_nt(key, q) * scale + bias
            expd = jnp.exp(scores - jnp.max(scores, axis=0, keepdims=True))
            probs = expd * (1.0 / jnp.sum(expd, axis=0, keepdims=True))
            pgrad = dot_nt(value, co)
            centre = jnp.sum(probs * pgrad, axis=0, keepdims=True)
            sgrad = (probs * (pgrad - centre) * scale).astype(jnp.bfloat16)
            vgrad = vgrad + jnp.dot(probs.astype(jnp.bfloat16), co, preferred_element_type=jnp.float32)
            rgrad = rgrad + jnp.dot(sgrad, q, preferred_element_type=jnp.float32)
        kgrad = rgrad * cosine[...] - pltpu.roll(rgrad * sine[...], HD // 2, 1) * sign
        klow, vlow = kgrad.astype(jnp.bfloat16), vgrad.astype(jnp.bfloat16)
        comb[:, pl.ds(2 * k * HD, HD)] = klow
        comb[:, pl.ds((2 * k + 1) * HD, HD)] = vlow
        cen = cen + jnp.sum(
            klow.astype(jnp.float32) * raw + vlow.astype(jnp.float32) * val,
            axis=1, keepdims=True,
        )
        for d in range(1, count):
            copy = piece_copy(d, k)
            copy.start()
            sent.append(copy)
        copy = remote(comb.at[:, pair(k)], poth.at[z, :, pair(k)], sb.at[0, k], rb.at[0, k], tensor=other)
        copy.start()
        sent.append(copy)
    cpart[...] = jnp.broadcast_to(cen, (toks, 128))
    ccopy = remote(cpart, cother, sc.at[0], rc.at[0], tensor=other)
    ccopy.start()
    pown[z] = comb[...]

    def cross_piece(d, k):
        place = lax.rem(z - d + count, count)
        return remote(
            pown.at[place, :, pair(k)], poth.at[place, :, pair(k)], sb.at[d, k], rb.at[d, k], tensor=other
        )

    for k in range(heads):
        for d in range(1, count):
            piece_copy(d, k).wait_recv()
            copy = cross_piece(d, k)
            copy.start()
            sent.append(copy)

    tile = min(half_rows, 256)

    def normed_grad(src, out, slot):
        def step(n, carry):
            mine = pl.ds(pl.multiple_of(y * half_rows + n * tile, 16), tile)
            at = pl.ds(pl.multiple_of(n * tile, 128), tile)
            a = dot_nt(pown[src], wcat[mine, :])
            b = dot_nt(poth[src], woth[at, :])
            both = a.astype(jnp.bfloat16).astype(jnp.float32) + b.astype(jnp.bfloat16).astype(jnp.float32)
            out[slot, :, at] = both.astype(jnp.bfloat16)
            return carry

        lax.fori_loop(0, half_rows // tile, step, 0)

    def wait_other(d):
        for k in range(heads):
            cross_piece(d, k).wait_recv()

    def grad_copy(c, d):
        at = pl.ds(c * chunk, chunk)
        return remote(
            ngs.at[d - 1, at, :], ngr.at[z, at, :], sn.at[c, d - 1], rn.at[c, d - 1],
            dp=lax.rem(z - d + count, count),
        )

    wcopy.wait()
    wait_other(0)
    normed_grad(z, ngr, z)
    for d in range(1, count):
        wait_other(d)
        normed_grad(lax.rem(z - d + count, count), ngs, d - 1)
        grad_copy(0, d).start()
    for d in range(1, count):
        grad_copy(1, d).start()
    ccopy.wait()

    wtile = min(rows, 256)
    wsteps = rows // wtile

    def weight_grad(n, carry):
        at = pl.ds(pl.multiple_of(n * wtile, 128), wtile)
        acc = jnp.zeros((wtile, 2 * kcols), jnp.float32)
        for r in range(count):
            term = dot_tn(cols[r, :, at], pown[r])
            acc = acc + term.astype(jnp.bfloat16).astype(jnp.float32)
        low_acc = acc.astype(jnp.bfloat16)
        for k in range(heads):
            head = pl.ds(k * HD, HD)
            kg_out[at, head] = low_acc[:, 2 * k * HD : (2 * k + 1) * HD]
            vg_out[at, head] = low_acc[:, (2 * k + 1) * HD : (2 * k + 2) * HD]
        return carry

    def out_place(c, w, which):
        feat = pl.ds(pl.multiple_of(w * rows + which * half_rows, 128), half_rows)
        return low.at[pl.ds(c * chunk, chunk), feat]

    def out_copy(c, w, to):
        src = cot.at[w, pl.ds(c * chunk, chunk), :]
        return remote(src, out_place(c, w, y), so.at[c, w, 0], ro.at[c, w, 0], pipe=to)

    def cross_copy(c, w, which):
        place = out_place(c, w, which)
        return remote(place, place, so.at[c, w, 1], ro.at[c, w, 1], tensor=other)

    first_staged = count // 2
    staging = has_lower & (lax.rem(p, 2) == 0)
    passes_all = has_upper & (lax.rem(p, 2) == 0)

    def stage_copy(c, w):
        at = pl.ds(c * chunk, chunk)
        i = w - first_staged
        return remote(
            cot.at[w, at, :], stage.at[i, at, :], sg.at[c, i], rg.at[c, i], tensor=other
        )

    def staged_out(c, w):
        i = w - first_staged
        return remote(
            stage.at[i, pl.ds(c * chunk, chunk), :], out_place(c, w, other),
            sh.at[c, i], ro.at[c, w, 1], pipe=p - 1,
        )

    def pass_on(c):
        @pl.when(staging)
        def _():
            for w in range(first_staged, count):
                stage_copy(c, w).wait_recv()
                staged_out(c, w).start()

        @pl.when(has_upper)
        def _():
            for w in range(count):
                out_copy(c, w, p + 1).wait_recv()
                if w < first_staged:
                    cross_copy(c, w, y).start()

        @pl.when(passes_all)
        def _():
            for w in range(first_staged, count):
                cross_copy(c, w, y).start()

    for c in range(BWD_CHUNKS):
        for d in range(1, count):
            grad_copy(c, d).wait_send()
            if c < BWD_CHUNKS - 2:
                grad_copy(c + 2, d).start()
        for d in range(1, count):
            grad_copy(c, d).wait_recv()

        def tail(i, carry):
            at = pl.ds(pl.multiple_of(c * chunk + i * 16, 16), 16)
            inv_rms = inv[at, :][:, :1]
            centre = (cpart[at, :] + cother[at, :])[:, :1] * (1.0 / width)
            for w in range(count):
                feat = pl.ds(pl.multiple_of(w * rows + y * half_rows, 128), half_rows)
                nhat = hid[at, feat].astype(jnp.float32) * inv_rms
                grad_in = ngr[w, at, :].astype(jnp.float32) * gain[:, feat]
                cot[w, at, :] = ((grad_in - nhat * centre) * inv_rms).astype(jnp.bfloat16)
            return carry

        lax.fori_loop(0, chunk // 16, tail, 0)

        @pl.when(has_lower)
        def _():
            for w in range(count):
                out_copy(c, w, p - 1).start()

        @pl.when(staging)
        def _():
            for w in range(first_staged, count):
                stage_copy(c, w).start()

        if c > 1:
            pass_on(c - 2)
        lax.fori_loop(wsteps * c // BWD_CHUNKS, wsteps * (c + 1) // BWD_CHUNKS, weight_grad, 0)

    pass_on(BWD_CHUNKS - 2)
    pass_on(BWD_CHUNKS - 1)

    for copy in sent:
        copy.wait_send()

    @pl.when(has_lower)
    def _():
        for c in range(BWD_CHUNKS):
            for w in range(count):
                out_copy(c, w, p - 1).wait_send()

    @pl.when(has_upper)
    def _():
        for c in range(BWD_CHUNKS):
            for w in range(count):
                if w < first_staged:
                    cross_copy(c, w, y).wait_send()
                cross_copy(c, w, other).wait_recv()

    @pl.when(passes_all)
    def _():
        for c in range(BWD_CHUNKS):
            for w in range(first_staged, count):
                cross_copy(c, w, y).wait_send()

    @pl.when(staging)
    def _():
        for c in range(BWD_CHUNKS):
            for w in range(first_staged, count):
                stage_copy(c, w).wait_send()
                staged_out(c, w).wait_send()


def section_call(arrays, count, stages):
    hidden, _, kw = arrays[:3]
    toks, width = hidden.shape
    rows = width // count
    kcols = kw.shape[1]
    heads = kcols // HD
    low, wide = jnp.bfloat16, jnp.float32
    vmem = pl.BlockSpec(memory_space=pltpu.VMEM)
    hbm = pl.BlockSpec(memory_space=pl.ANY)
    dma = pltpu.SemaphoreType.DMA
    m = toks // FWD_CHUNKS
    fpair = (FWD_CHUNKS, count - 1)
    bpair = (BWD_CHUNKS, count - 1)
    trio = (BWD_CHUNKS, count, 2)
    staged = (BWD_CHUNKS, count - count // 2)
    others = count - 1
    return pl.pallas_call(
        functools.partial(section_kernel, count, stages),
        out_shape=(
            jax.ShapeDtypeStruct((toks, width), low),
            jax.ShapeDtypeStruct((rows, kcols), low),
            jax.ShapeDtypeStruct((rows, kcols), low),
        ),
        in_specs=[vmem] * 10,
        out_specs=(hbm, vmem, vmem),
        scratch_shapes=[
            pltpu.VMEM((rows, 2 * kcols), low),
            pltpu.VMEM((toks, width), low),
            pltpu.VMEM((count, toks, rows), low),
            pltpu.VMEM((FWD_CHUNKS, m, 2 * kcols), wide),
            pltpu.VMEM((others, FWD_CHUNKS, m, 2 * kcols), low),
            pltpu.VMEM((others, FWD_CHUNKS, m, 2 * kcols), low),
            pltpu.VMEM((rows // 2, 2 * kcols), low),
            pltpu.VMEM((toks, 128), wide),
            pltpu.VMEM((toks, 2 * kcols), wide),
            pltpu.VMEM((toks, 2 * kcols), low),
            pltpu.VMEM((toks, 128), wide),
            pltpu.VMEM((count, toks, 2 * kcols), low),
            pltpu.VMEM((count, toks, 2 * kcols), low),
            pltpu.VMEM((others, toks, rows // 2), low),
            pltpu.VMEM((count, toks, rows // 2), low),
            pltpu.VMEM((count, toks, rows // 2), low),
            pltpu.VMEM((toks, 128), wide),
            pltpu.VMEM((count - count // 2, toks, rows // 2), low),
            dma(fpair), dma(fpair), dma((1,)), dma((1,)), dma(fpair), dma(fpair), dma(fpair), dma(fpair),
            dma((1,)),
            dma((others, heads)), dma((others, heads)), dma((count, heads)), dma((count, heads)), dma((1,)), dma((1,)),
            dma(bpair), dma(bpair), dma(trio), dma(trio), dma(staged), dma(staged), dma(staged),
        ],
        compiler_params=pltpu.CompilerParams(
            collective_id=0, has_side_effects=True, vmem_limit_bytes=VMEM_BYTES
        ),
        name="section",
    )(*arrays)


def on_device(
    hidden_states,
    norm_gain,
    key_weight,
    value_weight,
    queries,
    context_cotangent,
    lengths,
    policy_logp,
    reference_logp,
):
    count = lax.axis_size("dp")
    stages = lax.axis_size("pipe")
    hidden = hidden_states[0]
    toks = hidden.shape[0]
    assert lengths.shape[1] == 1 and lax.axis_size("tensor") == 2
    cosine, sine = rope_tables(toks, HD)
    seq_weight = 2.0 * jax.nn.sigmoid(npo_beta * (policy_logp[0] - reference_logp[0])) / count
    live = jnp.arange(toks)[:, None] < lengths[0][None, :]
    factor = jnp.where(live, seq_weight[None, :], 0.0)
    low, kg, vg = section_call(
        (
            hidden,
            norm_gain.astype(jnp.float32),
            key_weight[0],
            value_weight[0],
            queries[0],
            context_cotangent[0],
            jnp.broadcast_to(factor, (toks, 128)),
            jnp.broadcast_to(live.astype(jnp.float32), (toks, 128)),
            cosine,
            sine,
        ),
        count,
        stages,
    )
    low = jnp.where(lax.axis_index("pipe") < stages - 1, low, jnp.zeros_like(low))
    return (kg[None], vg[None], low[None])


def solution(mesh):
    in_specs = (
        P("pipe", "dp", None),
        P("pipe", None),
        P("pipe", "dp", "tensor"),
        P("pipe", "dp", "tensor"),
        P("pipe", "dp", "tensor"),
        P("pipe", "dp", "tensor"),
        P("pipe", "dp"),
        P("pipe", "dp"),
        P("pipe", "dp"),
    )
    out_specs = (P("pipe", "dp", "tensor"), P("pipe", "dp", "tensor"), P("pipe", "dp", None))
    return jax.shard_map(
        on_device, mesh=mesh, in_specs=in_specs, out_specs=out_specs, check_vma=False
    )
```
